128 devices in a mesh: seq: 8 (over x_lo, z), exp: 16 (over x_hi, y, core).
Axes of the slice: x: 4 (x_hi: 2, x_lo: 2; x = x_hi * 2 + x_lo), y: 4, z: 4, core: 2. Of those that a mesh axis runs over, the one named last changes fastest.
Arguments:
- queries: bfloat16 [64, 4096], P('exp'), may hold values from -80 to 80
- new_kv: bfloat16 [2, 64, 512], P(None, 'exp'), may hold values from -4 to 4
- kv_cache: bfloat16 [2, 64, 4096, 512], P(None, 'exp', 'seq'), may hold values from -4 to 4
- lengths: int32 [64], P('exp'), may hold values from 1 to 4096, as said below
- out_proj: bfloat16 [4096, 2048], P('seq'), may hold values from -0.09375 to 0.09375
- hidden_in: float32 [64, 2048], P('exp'), may hold values from -6 to 6
- norm_gain: float32 [2048], replicated, may hold values from 0.1 to 1.9
- router: bfloat16 [2048, 128], replicated, may hold values from -0.125 to 0.125
- expert_ids: int32 [64, 8], replicated, may hold values from 0 to 127, all different within a row; in each aligned block of 64 rows (0 to 63, 64 to 127, ...) at most 8 rows name the same one
- w_gate_up: bfloat16 [128, 2048, 1536], P(('seq', 'exp')), may hold values from -0.125 to 0.125
- w_down: bfloat16 [128, 768, 2048], P(('seq', 'exp')), may hold values from -0.21875 to 0.21875
- talk_proj: bfloat16 [2048, 1024], replicated, may hold values from -0.125 to 0.125
- talk_gain: float32 [1024], replicated, may hold values from 0.1 to 1.9
- talk_router: bfloat16 [1024, 128], replicated, may hold values from -0.1875 to 0.1875
- talk_ids: int32 [64, 8], replicated, may hold values from 0 to 127, all different within a row; in each aligned block of 64 rows (0 to 63, 64 to 127, ...) at most 8 rows name the same one
- talk_gate_up: bfloat16 [128, 1024, 768], P(('seq', 'exp')), may hold values from -0.1875 to 0.1875
- talk_down: bfloat16 [128, 384, 1024], P(('seq', 'exp')), may hold values from -0.3125 to 0.3125
Outputs:
- thinker_out: float32 [64, 2048], P('exp')
- talker_out: float32 [64, 1024], P('exp')
The draws below stay inside these ranges and needn't reach their ends.
Inputs may be any that keep to these rules, and one draw needn't show every extreme that they name: `lengths`: some conversation uses all 4096 positions and some uses only one. `expert_ids`: each row names 8 different experts. Over all 64 rows no expert is named more than 8 times, and in every draw some expert is named exactly 8 times. `talk_ids`: as for expert_ids.
All inputs are finite; a program needn't handle non-finite values.
Results may differ from the reference program's by a relative error of at most 0.011.
Values may be sent and summed in bfloat16 or wider, within the bound.
No kernel may reach another device: no remote copies, remote signals or barrier semaphores. Data moves between devices by JAX's collectives and lax.ppermute only.
A program may use at most 128 MiB of HBM per device.

```python
import math
import jax
import jax.numpy as jnp
import numpy as np
from jax import lax

D = 2048
H = 32
KVH = 4
HD = 128
FF = 768
TOP = 8
DT = 1024
FT = 384
EXPERTS = 128
CONVS = 64
CTX = 4096
CAP = 8


def shared_leading(key):
    return jnp.clip(jax.random.normal(jax.random.fold_in(key, 5), (CONVS, KVH * HD), jnp.float32), -4.0, 4.0)


def draw_kv_cache(key, part):
    leading = shared_leading(key)
    key = jax.random.fold_in(key, 11)
    entries = jnp.clip(jax.random.normal(key, (2, CONVS, CTX, KVH * HD), jnp.float32), -4.0, 4.0)
    entries = entries.at[0, :, 0, :].set(leading)
    direction = jax.random.uniform(jax.random.fold_in(key, 7), (CONVS, 1, KVH * HD), jnp.float32, -1.0, 1.0)
    position = (jnp.arange(CTX, dtype=jnp.float32) + 1.0) / CTX
    noise = 0.8 * entries[1]
    ramp = 0.1 + 1.9 * position
    values = jnp.clip(noise + ramp[None, :, None] * direction, -4.0, 4.0)
    entries = entries.at[1].set(values)
    return entries.astype(jnp.bfloat16)


def draw_queries(key, part):
    key = jax.random.fold_in(key, 23)
    values = jnp.clip(jax.random.normal(key, (CONVS, H * HD), jnp.float32), -4.0, 4.0)
    return values.astype(jnp.bfloat16)


def draw_lengths(key, part):
    key = jax.random.fold_in(key, 31)
    total_count = CONVS
    spans = jax.random.randint(jax.random.fold_in(key, 1), (total_count,), 1, CTX + 1, dtype=jnp.int32)
    longest = jax.random.randint(jax.random.fold_in(key, 2), (), 0, total_count, dtype=jnp.int32)
    offset = jax.random.randint(jax.random.fold_in(key, 3), (), 0, total_count - 1, dtype=jnp.int32)
    shortest = (longest + 1 + offset) % total_count
    spans = spans.at[longest].set(CTX).at[shortest].set(1)
    return spans


def block_levels(rng, extent, pieces, low, largest):
    def one(dim, shards_of):
        heights = jax.random.uniform(jax.random.fold_in(jax.random.fold_in(rng, 6), dim), (shards_of,), jnp.float32, low / len(pieces), largest / len(pieces))
        return jnp.repeat(jnp.exp(heights), extent[dim] // shards_of).reshape((-1,) + (1,) * (len(extent) - dim - 1))

    level = one(*pieces[0])
    for cut in pieces[1:]:
        level = level * one(*cut)
    return level


def deal_out(stream_key, own, number, rows, number_of, top, bound, slope):
    order = jax.random.permutation(stream_key, number_of)
    packed, usual = load_shares(number_of, rows * top, bound, slope, True), load_shares(number_of, rows * top, bound, slope, False)
    places = jnp.arange(number_of)

    def named(sizes, turn):
        used = int((sizes > 0).sum())
        fixed = max(1, used // 4)
        moved = fixed + (places - fixed + turn * (used - fixed)) % max(1, number_of - fixed)
        return jnp.zeros((number_of,), jnp.int32).at[order[jnp.where(places < fixed, places, moved)]].set(jnp.asarray(sizes, jnp.int32))

    sizes = jnp.where(number % 4 == 0, named(packed, number // 4), named(usual, number - number // 4 - 1))
    mixed = jax.random.permutation(jax.random.fold_in(own, 3), number_of)
    source_of, receiver = mixed[0:number_of // 2 * 2:2], mixed[1:number_of // 2 * 2:2]
    margin = jnp.minimum(sizes[source_of] - 1, bound - sizes[receiver]) // 2
    margin = jnp.where((source_of == order[0]) | (receiver == order[0]) | (sizes[receiver] == 0), 0, jnp.maximum(margin, 0))
    moved = jax.random.randint(jax.random.fold_in(own, 4), (number_of // 2,), 0, 1 << 20) % (margin + 1)
    sizes = sizes.at[source_of].add(-moved).at[receiver].add(moved)
    members = jnp.searchsorted(jnp.cumsum(sizes), jnp.arange(rows * top), side="right").astype(jnp.int32)
    grid = members.reshape(top, rows).T
    grid = grid[jax.random.permutation(jax.random.fold_in(own, 1), rows)]
    turn = jax.random.randint(jax.random.fold_in(own, 2), (rows, 1), 0, top)
    return jnp.take_along_axis(grid, (jnp.arange(top)[None, :] + turn) % top, axis=1)


def load_shares(number_of, total, limit, slope, full):
    portions = [(1 << 20) // math.isqrt(grade ** slope) + 1 for grade in range(1, number_of + 1)]
    largest = limit if full else min(limit, max(-(-total // number_of), total * portions[0] // sum(portions)))
    least = 1 if total - largest >= number_of - 1 else 0
    given, spare = [largest] + [least] * (number_of - 1), total - largest - least * (number_of - 1)
    while spare > 0:
        free = [i for i in range(1, number_of) if given[i] < largest] or [i for i in range(1, number_of) if given[i] < limit]
        pool, budget = sum([portions[i] for i in free]), spare
        for i in free:
            addition = min(limit - given[i], max(1, budget * portions[i] // pool), spare)
            given[i] = given[i] + addition
            spare = spare - addition
    return np.array(given)


def bell_draw(rng, extent, scale, limit, shards=(), kind=jnp.bfloat16):
    values = scale * jax.random.normal(rng, extent, jnp.float32)
    if shards:
        values = values * block_levels(rng, extent, shards, -0.22, 0.18)
    return jnp.clip(values, -limit, limit).astype(kind)


def setup_inputs(seed: int = 0) -> dict:
    splits = jax.random.split(jax.random.key(seed), 18)
    queries = draw_queries(jax.random.fold_in(splits[17], 71), 0)
    new_kv = bell_draw(splits[1], (2, CONVS, KVH * HD), 1.0, 4.0, ((1, 16),))
    kv_cache = draw_kv_cache(jax.random.fold_in(splits[17], 71), 0)
    lengths = draw_lengths(jax.random.fold_in(splits[17], 71), 0)
    out_proj = bell_draw(splits[4], (H * HD, D), (H * HD) ** -0.5, 0.09375, ((0, 8),))
    hidden_in = bell_draw(splits[5], (CONVS, D), 1.0, 6.0, ((0, 16),), jnp.float32)
    norm_gain = jnp.clip(1.0 + 0.18 * jax.random.normal(splits[6], (D,), jnp.float32), 0.1, 1.9)
    router = bell_draw(splits[7], (D, EXPERTS), D ** -0.5, 0.125)
    expert_ids_keys = jax.random.split(jax.random.fold_in(splits[8], 1), CONVS // CONVS)
    expert_ids_turns = jax.random.permutation(jax.random.fold_in(splits[8], 3), CONVS // CONVS)
    expert_ids = jax.vmap(lambda own, number: deal_out(jax.random.fold_in(splits[8], 2), own, number, CONVS, EXPERTS, TOP, CAP, 2))(expert_ids_keys, expert_ids_turns).reshape((CONVS, TOP))
    w_gate_up = bell_draw(splits[9], (EXPERTS, D, 2 * FF), D ** -0.5, 0.125, ((0, 128),))
    w_down = bell_draw(splits[10], (EXPERTS, FF, D), FF ** -0.5, 0.21875, ((0, 128),))
    talk_proj = bell_draw(splits[11], (D, DT), D ** -0.5, 0.125)
    talk_gain = jnp.clip(1.0 + 0.18 * jax.random.normal(splits[12], (DT,), jnp.float32), 0.1, 1.9)
    talk_router = bell_draw(splits[13], (DT, EXPERTS), DT ** -0.5, 0.1875)
    talk_ids_keys = jax.random.split(jax.random.fold_in(splits[14], 1), CONVS // CONVS)
    talk_ids_turns = jax.random.permutation(jax.random.fold_in(splits[14], 3), CONVS // CONVS)
    talk_ids = jax.vmap(lambda own, number: deal_out(jax.random.fold_in(splits[14], 2), own, number, CONVS, EXPERTS, TOP, CAP, 2))(talk_ids_keys, talk_ids_turns).reshape((CONVS, TOP))
    talk_gate_up = bell_draw(splits[15], (EXPERTS, DT, 2 * FT), DT ** -0.5, 0.1875, ((0, 128),))
    talk_down = bell_draw(splits[16], (EXPERTS, FT, DT), FT ** -0.5, 0.3125, ((0, 128),))
    return dict(queries=queries, new_kv=new_kv, kv_cache=kv_cache, lengths=lengths, out_proj=out_proj, hidden_in=hidden_in, norm_gain=norm_gain, router=router, expert_ids=expert_ids, w_gate_up=w_gate_up, w_down=w_down, talk_proj=talk_proj, talk_gain=talk_gain, talk_router=talk_router, talk_ids=talk_ids, talk_gate_up=talk_gate_up, talk_down=talk_down)


def attend_one(query_row, cached_keys, cached_values, fresh_key, fresh_value, length):
    groups = H // KVH
    query_f = query_row.reshape(KVH, groups, HD).astype(jnp.float32)
    keys = jnp.concatenate([cached_keys.reshape(CTX, KVH, HD), fresh_key.reshape(1, KVH, HD)], axis=0).astype(jnp.float32)
    values = jnp.concatenate([cached_values.reshape(CTX, KVH, HD), fresh_value.reshape(1, KVH, HD)], axis=0).astype(jnp.float32)
    scores = jnp.einsum('kjd,pkd->kjp', query_f, keys, precision=lax.Precision.HIGHEST) * HD ** (-0.5)
    valid = jnp.concatenate([jnp.arange(CTX, dtype=jnp.int32) < length, jnp.ones((1,), bool)], axis=0)
    scores = jnp.where(valid[None, None, :], scores, -jnp.inf)
    peak = lax.optimization_barrier(jnp.max(scores, axis=-1, keepdims=True))
    weights = jnp.exp(scores - peak)
    totals = lax.optimization_barrier(jnp.sum(weights, axis=-1))
    mixed = jnp.einsum('kjp,pkd->kjd', weights, values, precision=lax.Precision.HIGHEST)
    return (mixed / totals[..., None]).reshape(H * HD).astype(jnp.bfloat16)

def expert_layer(stream, gain, router_w, picks, gate_up, down_w):
    row_count, width = stream.shape
    top_count = picks.shape[1]
    inner_width = down_w.shape[1]
    normed = (stream * lax.rsqrt(lax.optimization_barrier(jnp.mean(stream * stream, axis=1, keepdims=True)) + 1e-06) * gain).astype(jnp.bfloat16)
    logits = jnp.dot(normed, router_w, preferred_element_type=jnp.float32)
    picked = jnp.take_along_axis(logits, picks, axis=1)
    sigmoids = jax.nn.sigmoid(picked)
    gates = sigmoids / lax.optimization_barrier(jnp.sum(sigmoids, axis=1, keepdims=True))
    flat_ids = picks.reshape(-1).astype(jnp.int32)

    def visit(totals, expert):
        hits = (flat_ids == expert).astype(jnp.int32)
        places = jnp.nonzero(flat_ids == expert, size=CAP, fill_value=0)[0].astype(jnp.int32)
        live = (jnp.arange(CAP, dtype=jnp.int32) < jnp.sum(hits)).astype(jnp.float32)
        chosen = normed[places // top_count]
        both = jnp.dot(chosen, gate_up[expert], preferred_element_type=jnp.float32)
        inner = (jax.nn.silu(both[:, :inner_width]) * both[:, inner_width:]).astype(jnp.bfloat16)
        replies = jnp.dot(inner, down_w[expert], preferred_element_type=jnp.float32).astype(jnp.bfloat16)
        replies = lax.optimization_barrier(replies).astype(jnp.float32)
        return (totals.at[places].add(replies * live[:, None]), None)
    start_totals = jnp.zeros((row_count * top_count, width), jnp.float32)
    totals, unused = lax.scan(visit, start_totals, jnp.arange(EXPERTS, dtype=jnp.int32))
    totals = totals.reshape(row_count, top_count, width)
    return stream + lax.optimization_barrier(jnp.sum(gates[:, :, None] * totals, axis=1))

def reference(queries, new_kv, kv_cache, lengths, out_proj, hidden_in, norm_gain, router, expert_ids, w_gate_up, w_down, talk_proj, talk_gain, talk_router, talk_ids, talk_gate_up, talk_down):

    def attend_items(items):
        return attend_one(items[0], items[1], items[2], items[3], items[4], items[5])
    attn = lax.map(attend_items, (queries, kv_cache[0], kv_cache[1], new_kv[0], new_kv[1], lengths))
    state = hidden_in + jnp.dot(attn, out_proj, preferred_element_type=jnp.float32)
    thinker = expert_layer(state, norm_gain, router, expert_ids, w_gate_up, w_down)
    talk_in = jnp.dot(thinker.astype(jnp.bfloat16), talk_proj, preferred_element_type=jnp.float32)
    talker = expert_layer(talk_in, talk_gain, talk_router, talk_ids, talk_gate_up, talk_down)
    return (thinker, talker)
```

```python
import functools
import jax
import jax.numpy as jnp
from jax import lax
from jax.experimental import pallas as pl
from jax.experimental.pallas import tpu as pltpu
from jax.sharding import PartitionSpec as P

F32 = jnp.float32
BF16 = jnp.bfloat16
HEADS = 32
KVH = 4
HD = 128
D = 2048
DT = 1024
FF = 768
FT = 384
EXPERTS = 128
ROWS = 64
SEQ = 8
EXP = 16
OWN = 4
SPAN = 512
EPS = 1e-6
NEG = -1e30


def iota(shape, dim):
    return lax.broadcasted_iota(jnp.int32, shape, dim)


def dot(a, b):
    return jnp.dot(a, b, preferred_element_type=F32)


def dot_t(a, b):
    return lax.dot_general(a, b, (((1,), (1,)), ((), ())), preferred_element_type=F32)


def start_all(pairs, sems):
    copies = []
    for k, (src, dst) in enumerate(pairs):
        copy = pltpu.make_async_copy(src, dst, sems.at[k])
        copy.start()
        copies.append(copy)
    return copies


def my_expert():
    return lax.axis_index("seq") * EXP + lax.axis_index("exp")


def slots_by_row(ids, me):
    eq = (ids == me).astype(F32)
    match = dot_t(jnp.ones((8, 8), F32), eq)
    before = (iota((ROWS, ROWS), 0) < iota((ROWS, ROWS), 1)).astype(F32)
    rank = dot(match, before)
    hit = jnp.logical_and(rank == iota((8, ROWS), 0).astype(F32), match > 0.5)
    return jnp.where(hit, 1.0, 0.0)


def rows_by_slot(ids, me, lanes):
    eq = (ids == me).astype(F32)
    match = dot(eq, jnp.ones((8, lanes), F32))
    before = (iota((ROWS, ROWS), 1) < iota((ROWS, ROWS), 0)).astype(F32)
    rank = dot(before, match)
    slot = jnp.bitwise_and(iota((ROWS, lanes), 1), 7).astype(F32)
    hit = jnp.logical_and(rank == slot, match > 0.5)
    return jnp.where(hit, 1.0, 0.0)


def spread_marks(count, bits, group=None):
    r = iota((ROWS, count), 0)
    i = iota((ROWS, count), 1)
    owner = i >> (2 + bits)
    if group is not None:
        owner = 2 * owner + group
    same = jnp.logical_and(owner == (r >> 2), (i & 3) == (r & 3))
    return jnp.where(same, 1.0, 0.0)


def spread_marks_t(count, bits, group=None):
    i = iota((count, ROWS), 0)
    r = iota((count, ROWS), 1)
    owner = i >> (2 + bits)
    if group is not None:
        owner = 2 * owner + group
    same = jnp.logical_and(owner == (r >> 2), (i & 3) == (r & 3))
    return jnp.where(same, 1.0, 0.0)


def by_chunk(marks, chunks):
    i = iota(marks.shape, 1)
    return jnp.concatenate(
        [jnp.where(((i >> 2) & (chunks - 1)) == j, marks, 0.0) for j in range(chunks)], axis=0
    )


def placing(ids, me, count, bits, group=None):
    chunks = 1 << bits
    lanes = 8 * chunks
    marks = dot(spread_marks_t(count, bits, group), rows_by_slot(ids, me, lanes))
    chunk = (iota((count, lanes), 0) >> 2) & (chunks - 1)
    return jnp.where((iota((count, lanes), 1) >> 3) == chunk, marks, 0.0).astype(BF16)


def pick_marks(slots, ids):
    lane = iota((ROWS, EXPERTS), 1)
    named = jnp.zeros((ROWS, EXPERTS), F32)
    for k in range(ids.shape[1]):
        named = named + (ids[:, k : k + 1] == lane).astype(F32)
    return dot(slots, named)


def gates_of(logits, picks, me):
    sig = 1.0 / (1.0 + jnp.exp(-logits))
    total = jnp.sum(sig * picks, axis=1, keepdims=True)
    own = jnp.sum(jnp.where(iota(sig.shape, 1) == me, sig, 0.0), axis=1, keepdims=True)
    return jnp.where(total > 0.0, own / total, 0.0)


def silu(a):
    return a / (1.0 + jnp.exp(-a))


def attend_kernel(len_ref, q_ref, new_ref, kv_ref, out_ref, k_buf, v_buf, q_buf, o_buf, t_buf, sems):
    pairs = []
    for c in range(OWN):
        pairs += [(kv_ref.at[0, c], k_buf.at[c]), (kv_ref.at[1, c], v_buf.at[c])]
    copies = start_all(pairs, sems)
    seq = lax.axis_index("seq")
    scale = HD ** (-0.5)
    query = q_ref[...].astype(F32)
    for h in range(HEADS):
        q_buf[4 * h : 4 * h + 4, :] = query[:, HD * h : HD * h + HD]
    lane = iota((HEADS, KVH * HD), 1)
    diag = (iota((HEADS, KVH * HD), 0) >> 3) == (lane >> 7)
    place = lane + seq * SPAN
    tail_lane = iota((HEADS, HD), 1)
    for c in range(OWN):
        q = q_buf[pl.ds(c, HEADS, stride=4), :]
        wide = jnp.where(diag, jnp.concatenate([q] * KVH, axis=1), 0.0)
        fresh_key = new_ref[0, c : c + 1, :].astype(F32)
        fresh_value = new_ref[1, c : c + 1, :].astype(F32)
        fresh = jnp.sum(wide * fresh_key, axis=1, keepdims=True) * scale
        fresh = jnp.where(seq == 0, fresh, NEG)
        copies[2 * c].wait()
        scores = dot_t(wide.astype(BF16), k_buf[c]) * scale
        valid = place < len_ref[c]
        scores = jnp.where(valid, scores, NEG)
        peak = jnp.maximum(jnp.max(scores, axis=1, keepdims=True), fresh)
        peak = peak.astype(BF16).astype(F32)
        weights = jnp.where(valid, jnp.exp(scores - peak), 0.0).astype(BF16)
        fresh_weight = jnp.where(seq == 0, jnp.exp(fresh - peak), 0.0)
        total = jnp.sum(weights.astype(F32), axis=1, keepdims=True) + fresh_weight
        copies[2 * c + 1].wait()
        mixed = dot(weights, v_buf[c]) + fresh_weight * fresh_value
        mixed = jnp.where(diag, mixed, 0.0)
        mixed = (mixed[:, :HD] + mixed[:, HD : 2 * HD]) + (
            mixed[:, 2 * HD : 3 * HD] + mixed[:, 3 * HD :]
        )
        upper = total.astype(BF16).astype(F32)
        tail = jnp.where(tail_lane == 0, peak, jnp.where(tail_lane == 1, upper, total - upper))
        o_buf[pl.ds(c, HEADS, stride=4), :] = mixed
        t_buf[pl.ds(c, HEADS, stride=4), :] = tail
    out_ref[:, :, :HD] = o_buf[...].reshape(SEQ, 16, HD).astype(BF16)
    out_ref[:, :, HD:] = t_buf[...].reshape(SEQ, 16, HD).astype(BF16)


def project_kernel(recv_ref, proj_ref, out_ref, p_buf, row_buf, sems):
    copies = start_all([(proj_ref, p_buf)], sems)
    got = recv_ref[...].astype(F32)
    peak = got[:, :, HD : HD + 1]
    total = got[:, :, HD + 1 : HD + 2] + got[:, :, HD + 2 : HD + 3]
    scale = jnp.exp(peak - jnp.max(peak, axis=0, keepdims=True))
    total = jnp.sum(scale * total, axis=0)
    mixed = jnp.sum(scale * got[:, :, :HD], axis=0) / total
    attn = jnp.concatenate([mixed[4 * h : 4 * h + 4] for h in range(4)], axis=1).astype(BF16)
    copies[0].wait()
    part = dot(attn, p_buf[...])
    for j in range(4):
        row_buf[4 * j : 4 * j + 4, :] = part[:, 512 * j : 512 * j + 512]
    msg = row_buf[...].astype(BF16)
    for d in range(SEQ):
        out_ref[d] = msg


def norm_kernel(recv_ref, hidden_ref, gain_ref, out_ref, state_ref, buf, gain_buf):
    for j in range(4):
        cols = slice(512 * j, 512 * j + 512)
        buf[4 * j : 4 * j + 4, :] = hidden_ref[:, cols]
        gain_buf[4 * j : 4 * j + 4, :] = jnp.broadcast_to(gain_ref[:, cols], (OWN, 512))
    state = buf[...] + jnp.sum(recv_ref[...].astype(F32), axis=0)
    square = jnp.sum(state * state, axis=1, keepdims=True)
    square = (square[0:4] + square[4:8]) + (square[8:12] + square[12:16])
    inv = lax.rsqrt(square * (1.0 / D) + EPS)
    normed = (state * jnp.concatenate([inv] * 4, axis=0) * gain_buf[...]).astype(BF16)
    for d in range(EXP):
        out_ref[d] = normed
    buf[...] = state
    for s in range(SEQ):
        for k in range(2):
            first = (s % 2) * 256 + k * 128
            state_ref[s, 4 * k : 4 * k + 4, :] = buf[4 * (s // 2) : 4 * (s // 2) + 4, first : first + 128]


def expert_kernel(
    recv_ref, ids_ref, router_ref, up_ref, down_ref, out_ref, r_buf, a_buf, b_buf, d_buf, sems
):
    parts = FF // 256
    pairs = [(router_ref, r_buf)]
    for f in range(parts):
        pairs += [
            (up_ref.at[0, :, pl.ds(256 * f, 256)], a_buf.at[f]),
            (up_ref.at[0, :, pl.ds(FF + 256 * f, 256)], b_buf.at[f]),
            (down_ref.at[0, pl.ds(256 * f, 256), :], d_buf.at[f]),
        ]
    copies = start_all(pairs, sems)
    me = my_expert()
    ids = ids_ref[...]
    slots = slots_by_row(ids, me)
    picks = pick_marks(slots, ids)
    place = placing(ids, me, 128, 1)
    chosen = by_chunk(dot(slots, spread_marks(256, 2)), 4).astype(BF16)
    rows = dot(chosen, recv_ref[...])
    rows = jnp.concatenate([rows[8 * j : 8 * j + 8] for j in range(4)], axis=1).astype(BF16)
    copies[0].wait()
    gates = gates_of(dot(rows, r_buf[...]), picks, me)
    reply = jnp.zeros((8, D), F32)
    for f in range(parts):
        copies[3 * f + 1].wait()
        a = dot(rows, a_buf[f])
        copies[3 * f + 2].wait()
        b = dot(rows, b_buf[f])
        inner = (silu(a) * b).astype(BF16)
        copies[3 * f + 3].wait()
        reply = reply + dot(inner, d_buf[f])
    reply = gates * reply.astype(BF16).astype(F32)
    halves = [
        jnp.concatenate(
            [reply[:, 256 * s + 128 * k : 256 * s + 128 * k + 128] for s in range(SEQ)], axis=1
        )
        for k in range(2)
    ]
    sent = dot(place, jnp.concatenate(halves, axis=0).astype(BF16))
    for s in range(SEQ):
        block = sent[:, 128 * s : 128 * s + 128].reshape(EXP, 8, 128)
        out_ref[EXP * s : EXP * s + EXP] = block.astype(BF16)


def total_kernel(recv_ref, state_ref, out_ref):
    total = jnp.sum(recv_ref[...].astype(F32), axis=0) + state_ref[lax.axis_index("seq")]
    out_ref[...] = jnp.broadcast_to(total.astype(BF16)[None], out_ref.shape)


def talker_kernel(
    recv_ref,
    ids_ref,
    gain_ref,
    proj_ref,
    router_ref,
    up_ref,
    down_ref,
    thinker_ref,
    talk_ref,
    keep_ref,
    give_ref,
    p_buf,
    r_buf,
    u_buf,
    d_buf,
    sems,
):
    pairs = [(proj_ref.at[pl.ds(512 * q, 512), :], p_buf.at[q]) for q in range(4)]
    pairs += [(router_ref, r_buf), (up_ref.at[0], u_buf), (down_ref.at[0], d_buf)]
    copies = start_all(pairs, sems)
    me = my_expert()
    group = lax.axis_index("exp")
    core = group & 1
    ids = ids_ref[...]
    slots = slots_by_row(ids, me)
    picks = pick_marks(slots, ids)
    keep_place = placing(ids, me, 128, 2, core)
    give_place = placing(ids, me, 128, 2, 1 - core)
    slot = iota((8, ROWS), 0)
    own = jnp.logical_and(iota((8, ROWS), 1) == OWN * group + slot, slot < OWN)
    wanted = jnp.concatenate([slots, jnp.where(own, 1.0, 0.0)], axis=0)
    chosen = by_chunk(dot(wanted, spread_marks(128, 1)), 2).astype(BF16)
    talk_in = jnp.zeros((16, DT), F32)
    for q in range(4):
        cols = []
        for s in (2 * q, 2 * q + 1):
            got = dot(chosen, recv_ref[128 * s : 128 * s + 128, :])
            cols += [got[:16], got[16:]]
        part = jnp.concatenate(cols, axis=1)
        thinker_ref[:, 512 * q : 512 * q + 512] = part[8 : 8 + OWN]
        copies[q].wait()
        talk_in = talk_in + dot(part.astype(BF16), p_buf[q])
    talk_ref[...] = talk_in[8 : 8 + OWN]
    talk_in = talk_in[:8]
    mean = jnp.mean(talk_in * talk_in, axis=1, keepdims=True)
    normed = (talk_in * lax.rsqrt(mean + EPS) * gain_ref[...]).astype(BF16)
    copies[4].wait()
    gates = gates_of(dot(normed, r_buf[...]), picks, me)
    copies[5].wait()
    both = dot(normed, u_buf[...])
    inner = (silu(both[:, :FT]) * both[:, FT:]).astype(BF16)
    copies[6].wait()
    reply = gates * dot(inner, d_buf[...]).astype(BF16).astype(F32)
    stacked = jnp.concatenate([reply[:, 256 * j : 256 * j + 256] for j in range(4)], axis=0)
    stacked = stacked.astype(BF16)
    keep_ref[...] = dot(keep_place, stacked).reshape(8, 16, 256).astype(BF16)
    give_ref[...] = dot(give_place, stacked).reshape(8, 16, 256).astype(BF16)


def pair_kernel(keep_ref, got_ref, out_ref):
    total = (keep_ref[...].astype(F32) + got_ref[...].astype(F32)).astype(BF16)
    for s in range(SEQ):
        out_ref[8 * s : 8 * s + 8] = total


def finish_kernel(recv_ref, talk_ref, out_ref, buf):
    buf[...] = jnp.sum(recv_ref[...].astype(F32), axis=0)
    for j in range(4):
        cols = slice(256 * j, 256 * j + 256)
        out_ref[:, cols] = talk_ref[:, cols] + buf[4 * j : 4 * j + 4, :]


def call(kernel, outs, args, where, scratch=(), mib=16):
    spaces = {"v": pltpu.VMEM, "s": pltpu.SMEM, "h": pl.ANY}
    many = isinstance(outs, list)
    whole = pl.BlockSpec(memory_space=pltpu.VMEM)
    return pl.pallas_call(
        kernel,
        out_shape=outs,
        in_specs=[pl.BlockSpec(memory_space=spaces[w]) for w in where],
        out_specs=[whole] * len(outs) if many else whole,
        scratch_shapes=list(scratch),
        compiler_params=pltpu.CompilerParams(vmem_limit_bytes=mib << 20),
    )(*args)


def array(shape, dtype):
    return jax.ShapeDtypeStruct(shape, dtype)


def exchange(msg, axis, groups=None):
    return lax.all_to_all(msg, axis, 0, 0, axis_index_groups=groups)


def on_device(
    queries,
    new_kv,
    kv_cache,
    lengths,
    out_proj,
    hidden_in,
    norm_gain,
    router,
    expert_ids,
    w_gate_up,
    w_down,
    talk_proj,
    talk_gain,
    talk_router,
    talk_ids,
    talk_gate_up,
    talk_down,
):
    both = ("seq", "exp")
    dma = pltpu.SemaphoreType.DMA
    msg = call(
        attend_kernel,
        array((SEQ, 16, 256), BF16),
        (lengths, queries, new_kv, kv_cache),
        "svvh",
        [
            pltpu.VMEM((OWN, SPAN, KVH * HD), BF16),
            pltpu.VMEM((OWN, SPAN, KVH * HD), BF16),
            pltpu.VMEM((HEADS * OWN, HD), F32),
            pltpu.VMEM((HEADS * OWN, HD), F32),
            pltpu.VMEM((HEADS * OWN, HD), F32),
            dma((2 * OWN,)),
        ],
    )
    msg = call(
        project_kernel,
        array((SEQ, 16, 512), BF16),
        (exchange(msg, "seq"), out_proj),
        "vh",
        [pltpu.VMEM((512, D), BF16), pltpu.VMEM((16, 512), F32), dma((1,))],
    )
    msg, state = call(
        norm_kernel,
        [array((EXP, 16, 512), BF16), array((SEQ, 8, 128), F32)],
        (exchange(msg, "seq"), hidden_in, norm_gain.reshape(1, D)),
        "vvv",
        [pltpu.VMEM((16, 512), F32), pltpu.VMEM((16, 512), F32)],
    )
    msg = call(
        expert_kernel,
        array((SEQ * EXP, 8, 128), BF16),
        (exchange(msg, "exp").reshape(256, 512), expert_ids, router, w_gate_up, w_down),
        "vvhhh",
        [
            pltpu.VMEM((D, EXPERTS), BF16),
            pltpu.VMEM((FF // 256, D, 256), BF16),
            pltpu.VMEM((FF // 256, D, 256), BF16),
            pltpu.VMEM((FF // 256, 256, D), BF16),
            dma((1 + 3 * (FF // 256),)),
        ],
    )
    msg = call(
        total_kernel,
        array((SEQ * EXP, 8, 128), BF16),
        (exchange(msg, both), state),
        "vv",
    )
    thinker, talk_in, keep, give = call(
        talker_kernel,
        [
            array((OWN, D), F32),
            array((OWN, DT), F32),
            array((8, 16, 256), BF16),
            array((8, 16, 256), BF16),
        ],
        (
            exchange(msg, both).reshape(1024, 128),
            talk_ids,
            talk_gain.reshape(1, DT),
            talk_proj,
            talk_router,
            talk_gate_up,
            talk_down,
        ),
        "vvvhhhh",
        [
            pltpu.VMEM((4, 512, DT), BF16),
            pltpu.VMEM((DT, EXPERTS), BF16),
            pltpu.VMEM((DT, 2 * FT), BF16),
            pltpu.VMEM((FT, DT), BF16),
            dma((7,)),
        ],
    )
    got = lax.ppermute(give, "exp", [(e, e ^ 1) for e in range(EXP)])
    msg = call(pair_kernel, array((64, 16, 256), BF16), (keep, got), "vv")
    same_core = [[2 * i + core for i in range(64)] for core in range(2)]
    talker = call(
        finish_kernel,
        array((OWN, DT), F32),
        (exchange(msg, both, same_core), talk_in),
        "vv",
        [pltpu.VMEM((16, 256), F32)],
    )
    return (thinker, talker)


def solution(mesh):
    placed = (
        P("exp", None),
        P(None, "exp", None),
        P(None, "exp", "seq", None),
        P("exp"),
        P("seq", None),
        P("exp", None),
        P(),
        P(),
        P(),
        P(("seq", "exp"), None, None),
        P(("seq", "exp"), None, None),
        P(),
        P(),
        P(),
        P(),
        P(("seq", "exp"), None, None),
        P(("seq", "exp"), None, None),
    )
    return jax.shard_map(
        on_device,
        mesh=mesh,
        in_specs=placed,
        out_specs=(P("exp", None), P("exp", None)),
        check_vma=False,
    )
```

```python
import functools
import jax
import jax.numpy as jnp
from jax import lax
from jax.experimental import pallas as pl
from jax.experimental.pallas import tpu as pltpu
from jax.sharding import PartitionSpec as P

F32 = jnp.float32
BF16 = jnp.bfloat16
HEADS = 32
KVH = 4
HD = 128
D = 2048
DT = 1024
FF = 768
FT = 384
EXPERTS = 128
ROWS = 64
SEQ = 8
EXP = 16
OWN = 4
SPAN = 512
EPS = 1e-6
COST = 10**11
NEG = -1e30


def iota(shape, dim):
    return lax.broadcasted_iota(jnp.int32, shape, dim)


def dot(a, b):
    return jnp.dot(a, b, preferred_element_type=F32)


def dot_t(a, b):
    return lax.dot_general(a, b, (((1,), (1,)), ((), ())), preferred_element_type=F32)


def my_expert():
    return lax.axis_index("seq") * EXP + lax.axis_index("exp")


def slots_by_row(ids, me):
    match = jnp.sum((ids == me).astype(F32), axis=0, keepdims=True)
    match = jnp.broadcast_to(match, (8, ROWS))
    before = (iota((ROWS, ROWS), 0) < iota((ROWS, ROWS), 1)).astype(F32)
    rank = dot(match, before)
    hit = jnp.logical_and(rank == iota((8, ROWS), 0).astype(F32), match > 0.5)
    return jnp.where(hit, 1.0, 0.0)


def spread_marks(count, bits, group=None):
    r = iota((ROWS, count), 0)
    i = iota((ROWS, count), 1)
    owner = i >> (2 + bits)
    if group is not None:
        owner = 2 * owner + group
    same = jnp.logical_and(owner == (r >> 2), (i & 3) == (r & 3))
    return jnp.where(same, 1.0, 0.0)


def spread_marks_t(count, bits, group=None):
    i = iota((count, ROWS), 0)
    r = iota((count, ROWS), 1)
    owner = i >> (2 + bits)
    if group is not None:
        owner = 2 * owner + group
    same = jnp.logical_and(owner == (r >> 2), (i & 3) == (r & 3))
    return jnp.where(same, 1.0, 0.0)


def by_chunk(marks, chunks):
    i = iota(marks.shape, 1)
    return jnp.concatenate(
        [jnp.where(((i >> 2) & (chunks - 1)) == j, marks, 0.0) for j in range(chunks)], axis=0
    )


def placing(slots, count, bits, group=None):
    chunks = 1 << bits
    lanes = 8 * chunks
    marks = dot_t(spread_marks_t(count, bits, group), jnp.concatenate([slots] * chunks, axis=0))
    chunk = (iota((count, lanes), 0) >> 2) & (chunks - 1)
    return jnp.where((iota((count, lanes), 1) >> 3) == chunk, marks, 0.0).astype(BF16)


def pick_marks(slots, ids):
    expert = iota((EXPERTS, ROWS), 0)
    named = jnp.zeros((EXPERTS, ROWS), F32)
    for k in range(ids.shape[0]):
        named = named + (ids[k : k + 1, :] == expert).astype(F32)
    return dot_t(slots, named)


def gates_of(logits, picks, me):
    sig = 1.0 / (1.0 + jnp.exp(-logits))
    total = jnp.sum(sig * picks, axis=1, keepdims=True)
    own = jnp.sum(jnp.where(iota(sig.shape, 1) == me, sig, 0.0), axis=1, keepdims=True)
    return jnp.where(total > 0.0, own / total, 0.0)


def silu(a):
    return a / (1.0 + jnp.exp(-a))


def start_all(pairs, sems):
    copies = []
    for k, (src, dst) in enumerate(pairs):
        copy = pltpu.make_async_copy(src, dst, sems.at[k])
        copy.start()
        copies.append(copy)
    return copies


def attend_kernel(
    len_hbm, q_hbm, new_hbm, kv_hbm, out_ref, len_ref, q_ref, new_ref, kv_ref, q_buf, o_buf, t_buf, sems
):
    pairs = [(q_hbm, q_ref), (new_hbm, new_ref), (len_hbm, len_ref)]
    for c in range(OWN):
        pairs += [(kv_hbm.at[t, c], kv_ref.at[t, c]) for t in range(2)]
    copies = start_all(pairs, sems)
    for copy in copies[:3]:
        copy.wait()
    seq = lax.axis_index("seq")
    scale = HD ** (-0.5)
    query = q_ref[...].astype(F32)
    for h in range(HEADS):
        q_buf[4 * h : 4 * h + 4, :] = query[:, HD * h : HD * h + HD]
    lane = iota((HEADS, KVH * HD), 1)
    diag = (iota((HEADS, KVH * HD), 0) >> 3) == (lane >> 7)
    place = lane + seq * SPAN
    tail_lane = iota((HEADS, HD), 1)
    for c in range(OWN):
        q = q_buf[pl.ds(c, HEADS, stride=4), :]
        wide = jnp.where(diag, jnp.concatenate([q] * KVH, axis=1), 0.0)
        fresh_key = new_ref[0, c : c + 1, :].astype(F32)
        fresh_value = new_ref[1, c : c + 1, :].astype(F32)
        fresh = jnp.sum(wide * fresh_key, axis=1, keepdims=True) * scale
        fresh = jnp.where(seq == 0, fresh, NEG)
        copies[2 * c + 3].wait()
        scores = dot_t(wide.astype(BF16), kv_ref[0, c]) * scale
        valid = place < len_ref[c]
        scores = jnp.where(valid, scores, NEG)
        peak = jnp.maximum(jnp.max(scores, axis=1, keepdims=True), fresh)
        peak = peak.astype(BF16).astype(F32)
        weights = jnp.where(valid, jnp.exp(scores - peak), 0.0).astype(BF16)
        fresh_weight = jnp.where(seq == 0, jnp.exp(fresh - peak), 0.0)
        total = jnp.sum(weights.astype(F32), axis=1, keepdims=True) + fresh_weight
        copies[2 * c + 4].wait()
        mixed = dot(weights, kv_ref[1, c]) + fresh_weight * fresh_value
        mixed = jnp.where(diag, mixed, 0.0)
        mixed = (mixed[:, :HD] + mixed[:, HD : 2 * HD]) + (
            mixed[:, 2 * HD : 3 * HD] + mixed[:, 3 * HD :]
        )
        upper = total.astype(BF16).astype(F32)
        tail = jnp.where(tail_lane == 0, peak, jnp.where(tail_lane == 1, upper, total - upper))
        o_buf[pl.ds(c, HEADS, stride=4), :] = mixed
        t_buf[pl.ds(c, HEADS, stride=4), :] = tail
    out_ref[:, :, :HD] = o_buf[...].reshape(SEQ, 16, HD).astype(BF16)
    out_ref[:, :, HD:] = t_buf[...].reshape(SEQ, 16, HD).astype(BF16)


def project_kernel(recv_ref, proj_ref, out_ref, row_buf):
    got = recv_ref[...].astype(F32)
    peak = got[:, :, HD : HD + 1]
    total = got[:, :, HD + 1 : HD + 2] + got[:, :, HD + 2 : HD + 3]
    scale = jnp.exp(peak - jnp.max(peak, axis=0, keepdims=True))
    total = jnp.sum(scale * total, axis=0)
    mixed = jnp.sum(scale * got[:, :, :HD], axis=0) / total
    attn = jnp.concatenate([mixed[4 * h : 4 * h + 4] for h in range(4)], axis=1).astype(BF16)
    part = dot(attn, proj_ref[...])
    for j in range(4):
        row_buf[4 * j : 4 * j + 4, :] = part[:, 512 * j : 512 * j + 512]
    msg = row_buf[...].astype(BF16)
    for d in range(SEQ):
        out_ref[d] = msg


def norm_kernel(recv_ref, hidden_ref, gain_ref, out_ref, state_ref, buf, gain_buf):
    for j in range(4):
        cols = slice(512 * j, 512 * j + 512)
        buf[4 * j : 4 * j + 4, :] = hidden_ref[:, cols]
        gain_buf[4 * j : 4 * j + 4, :] = jnp.broadcast_to(gain_ref[:, cols], (OWN, 512))
    state = buf[...] + jnp.sum(recv_ref[...].astype(F32), axis=0)
    square = jnp.sum(state * state, axis=1, keepdims=True)
    square = (square[0:4] + square[4:8]) + (square[8:12] + square[12:16])
    inv = lax.rsqrt(square * (1.0 / D) + EPS)
    normed = (state * jnp.concatenate([inv] * 4, axis=0) * gain_buf[...]).astype(BF16)
    for d in range(EXP):
        out_ref[d] = normed
    buf[...] = state
    for s in range(SEQ):
        for k in range(2):
            first = (s % 2) * 256 + k * 128
            state_ref[s, 4 * k : 4 * k + 4, :] = buf[4 * (s // 2) : 4 * (s // 2) + 4, first : first + 128]


def expert_kernel(recv_ref, ids_ref, router_ref, up_ref, down_ref, out_ref):
    me = my_expert()
    ids = ids_ref[...]
    slots = slots_by_row(ids, me)
    picks = pick_marks(slots, ids)
    place = placing(slots, 128, 1)
    chosen = by_chunk(dot(slots, spread_marks(256, 2)), 4).astype(BF16)
    rows = dot(chosen, recv_ref[...])
    rows = jnp.concatenate([rows[8 * j : 8 * j + 8] for j in range(4)], axis=1).astype(BF16)
    gates = gates_of(dot(rows, router_ref[...]), picks, me)
    both = dot(rows, up_ref[0])
    inner = (silu(both[:, :FF]) * both[:, FF:]).astype(BF16)
    reply = dot(inner, down_ref[0])
    reply = gates * reply.astype(BF16).astype(F32)
    halves = [
        jnp.concatenate(
            [reply[:, 256 * s + 128 * k : 256 * s + 128 * k + 128] for s in range(SEQ)], axis=1
        )
        for k in range(2)
    ]
    sent = dot(place, jnp.concatenate(halves, axis=0).astype(BF16))
    for s in range(SEQ):
        block = sent[:, 128 * s : 128 * s + 128].reshape(EXP, 8, 128)
        out_ref[EXP * s : EXP * s + EXP] = block.astype(BF16)


def total_kernel(recv_ref, state_ref, out_ref):
    total = jnp.sum(recv_ref[...].astype(F32), axis=0) + state_ref[lax.axis_index("seq")]
    out_ref[...] = jnp.broadcast_to(total.astype(BF16)[None], out_ref.shape)


def talker_kernel(
    recv_ref,
    ids_ref,
    gain_ref,
    proj_ref,
    router_ref,
    up_ref,
    down_ref,
    thinker_ref,
    talk_ref,
    keep_ref,
    give_ref,
):
    me = my_expert()
    group = lax.axis_index("exp")
    core = group & 1
    ids = ids_ref[...]
    slots = slots_by_row(ids, me)
    picks = pick_marks(slots, ids)
    keep_place = placing(slots, 128, 2, core)
    give_place = placing(slots, 128, 2, 1 - core)
    slot = iota((8, ROWS), 0)
    own = jnp.logical_and(iota((8, ROWS), 1) == OWN * group + slot, slot < OWN)
    wanted = jnp.concatenate([slots, jnp.where(own, 1.0, 0.0)], axis=0)
    chosen = by_chunk(dot(wanted, spread_marks(128, 1)), 2).astype(BF16)
    talk_in = jnp.zeros((16, DT), F32)
    for q in range(4):
        cols = []
        for s in (2 * q, 2 * q + 1):
            got = dot(chosen, recv_ref[128 * s : 128 * s + 128, :])
            cols += [got[:16], got[16:]]
        part = jnp.concatenate(cols, axis=1)
        thinker_ref[:, 512 * q : 512 * q + 512] = part[8 : 8 + OWN]
        talk_in = talk_in + dot(part.astype(BF16), proj_ref[512 * q : 512 * q + 512, :])
    talk_ref[...] = talk_in[8 : 8 + OWN]
    talk_in = talk_in[:8]
    mean = jnp.mean(talk_in * talk_in, axis=1, keepdims=True)
    normed = (talk_in * lax.rsqrt(mean + EPS) * gain_ref[...]).astype(BF16)
    gates = gates_of(dot(normed, router_ref[...]), picks, me)
    both = dot(normed, up_ref[0])
    inner = (silu(both[:, :FT]) * both[:, FT:]).astype(BF16)
    reply = gates * dot(inner, down_ref[0]).astype(BF16).astype(F32)
    stacked = jnp.concatenate([reply[:, 256 * j : 256 * j + 256] for j in range(4)], axis=0)
    stacked = stacked.astype(BF16)
    keep_ref[...] = dot(keep_place, stacked).reshape(8, 16, 256).astype(BF16)
    give_ref[...] = dot(give_place, stacked).reshape(8, 16, 256).astype(BF16)


def pair_kernel(keep_ref, got_ref, out_ref):
    total = (keep_ref[...].astype(F32) + got_ref[...].astype(F32)).astype(BF16)
    for s in range(SEQ):
        out_ref[8 * s : 8 * s + 8] = total


def finish_kernel(recv_ref, talk_ref, out_ref, buf):
    buf[...] = jnp.sum(recv_ref[...].astype(F32), axis=0)
    for j in range(4):
        cols = slice(256 * j, 256 * j + 256)
        out_ref[:, cols] = talk_ref[:, cols] + buf[4 * j : 4 * j + 4, :]


def call(kernel, outs, args, where, scratch=(), mib=16, flops=COST):
    spaces = {"v": pltpu.VMEM, "s": pltpu.SMEM, "h": pltpu.HBM}
    many = isinstance(outs, list)
    whole = pl.BlockSpec(memory_space=pltpu.VMEM)
    return pl.pallas_call(
        kernel,
        out_shape=outs,
        in_specs=[pl.BlockSpec(memory_space=spaces[w]) for w in where],
        out_specs=[whole] * len(outs) if many else whole,
        scratch_shapes=list(scratch),
        cost_estimate=pl.CostEstimate(flops=flops, bytes_accessed=1 << 20, transcendentals=0),
        compiler_params=pltpu.CompilerParams(vmem_limit_bytes=mib << 20),
    )(*args)


def array(shape, dtype):
    return jax.ShapeDtypeStruct(shape, dtype)


def exchange(msg, axis, groups=None):
    return lax.all_to_all(msg, axis, 0, 0, axis_index_groups=groups)


def on_device(
    queries,
    new_kv,
    kv_cache,
    lengths,
    out_proj,
    hidden_in,
    norm_gain,
    router,
    expert_ids,
    w_gate_up,
    w_down,
    talk_proj,
    talk_gain,
    talk_router,
    talk_ids,
    talk_gate_up,
    talk_down,
):
    both = ("seq", "exp")
    msg = call(
        attend_kernel,
        array((SEQ, 16, 256), BF16),
        (lengths, queries, new_kv, kv_cache),
        "hhhh",
        [
            pltpu.SMEM((OWN,), jnp.int32),
            pltpu.VMEM((OWN, HEADS * HD), BF16),
            pltpu.VMEM((2, OWN, KVH * HD), BF16),
            pltpu.VMEM((2, OWN, SPAN, KVH * HD), BF16),
            pltpu.VMEM((HEADS * OWN, HD), F32),
            pltpu.VMEM((HEADS * OWN, HD), F32),
            pltpu.VMEM((HEADS * OWN, HD), F32),
            pltpu.SemaphoreType.DMA((3 + 2 * OWN,)),
        ],
        mib=60,
    )
    msg = call(
        project_kernel,
        array((SEQ, 16, 512), BF16),
        (exchange(msg, "seq"), out_proj),
        "vv",
        [pltpu.VMEM((16, 512), F32)],
    )
    msg, state = call(
        norm_kernel,
        [array((EXP, 16, 512), BF16), array((SEQ, 8, 128), F32)],
        (exchange(msg, "seq"), hidden_in, norm_gain.reshape(1, D)),
        "vvv",
        [pltpu.VMEM((16, 512), F32), pltpu.VMEM((16, 512), F32)],
    )
    msg = call(
        expert_kernel,
        array((SEQ * EXP, 8, 128), BF16),
        (exchange(msg, "exp").reshape(256, 512), expert_ids.T, router, w_gate_up, w_down),
        "vvvvv",
    )
    msg = call(
        total_kernel,
        array((SEQ * EXP, 8, 128), BF16),
        (exchange(msg, both), state),
        "vv",
    )
    thinker, talk_in, keep, give = call(
        talker_kernel,
        [
            array((OWN, D), F32),
            array((OWN, DT), F32),
            array((8, 16, 256), BF16),
            array((8, 16, 256), BF16),
        ],
        (
            exchange(msg, both).reshape(1024, 128),
            talk_ids.T,
            talk_gain.reshape(1, DT),
            talk_proj,
            talk_router,
            talk_gate_up,
            talk_down,
        ),
        "vvvvvvv",
    )
    got = lax.ppermute(give, "exp", [(e, e ^ 1) for e in range(EXP)])
    msg = call(pair_kernel, array((64, 16, 256), BF16), (keep, got), "vv")
    same_core = [[2 * i + core for i in range(64)] for core in range(2)]
    talker = call(
        finish_kernel,
        array((OWN, DT), F32),
        (exchange(msg, both, same_core), talk_in),
        "vv",
        [pltpu.VMEM((16, 256), F32)],
    )
    return (thinker, talker)


def solution(mesh):
    placed = (
        P("exp", None),
        P(None, "exp", None),
        P(None, "exp", "seq", None),
        P("exp"),
        P("seq", None),
        P("exp", None),
        P(),
        P(),
        P(),
        P(("seq", "exp"), None, None),
        P(("seq", "exp"), None, None),
        P(),
        P(),
        P(),
        P(),
        P(("seq", "exp"), None, None),
        P(("seq", "exp"), None, None),
    )
    return jax.shard_map(
        on_device,
        mesh=mesh,
        in_specs=placed,
        out_specs=(P("exp", None), P("exp", None)),
        check_vma=False,
    )
```

```python
import functools
import jax
import jax.numpy as jnp
from jax import lax
from jax.experimental import pallas as pl
from jax.experimental.pallas import tpu as pltpu
from jax.sharding import PartitionSpec as P

F32 = jnp.float32
BF16 = jnp.bfloat16
HEADS = 32
KVH = 4
HD = 128
D = 2048
DT = 1024
FF = 768
FT = 384
EXPERTS = 128
ROWS = 64
SEQ = 8
EXP = 16
OWN = 4
SPAN = 512
EPS = 1e-6
COST = 10**11
NEG = -1e30


def iota(shape, dim):
    return lax.broadcasted_iota(jnp.int32, shape, dim)


def dot(a, b):
    return jnp.dot(a, b, preferred_element_type=F32)


def dot_t(a, b):
    return lax.dot_general(a, b, (((1,), (1,)), ((), ())), preferred_element_type=F32)


def my_expert():
    return lax.axis_index("seq") * EXP + lax.axis_index("exp")


def slots_by_row(ids, me):
    match = jnp.sum((ids == me).astype(F32), axis=0, keepdims=True)
    match = jnp.broadcast_to(match, (8, ROWS))
    before = (iota((ROWS, ROWS), 0) < iota((ROWS, ROWS), 1)).astype(F32)
    rank = dot(match, before)
    hit = jnp.logical_and(rank == iota((8, ROWS), 0).astype(F32), match > 0.5)
    return jnp.where(hit, 1.0, 0.0)


def spread_marks(count, bits, group=None):
    r = iota((ROWS, count), 0)
    i = iota((ROWS, count), 1)
    owner = i >> (2 + bits)
    if group is not None:
        owner = 2 * owner + group
    same = jnp.logical_and(owner == (r >> 2), (i & 3) == (r & 3))
    return jnp.where(same, 1.0, 0.0)


def spread_marks_t(count, bits, group=None):
    i = iota((count, ROWS), 0)
    r = iota((count, ROWS), 1)
    owner = i >> (2 + bits)
    if group is not None:
        owner = 2 * owner + group
    same = jnp.logical_and(owner == (r >> 2), (i & 3) == (r & 3))
    return jnp.where(same, 1.0, 0.0)


def by_chunk(marks, chunks):
    i = iota(marks.shape, 1)
    return jnp.concatenate(
        [jnp.where(((i >> 2) & (chunks - 1)) == j, marks, 0.0) for j in range(chunks)], axis=0
    )


def placing(slots, count, bits, group=None):
    chunks = 1 << bits
    lanes = 8 * chunks
    marks = dot_t(spread_marks_t(count, bits, group), jnp.concatenate([slots] * chunks, axis=0))
    chunk = (iota((count, lanes), 0) >> 2) & (chunks - 1)
    return jnp.where((iota((count, lanes), 1) >> 3) == chunk, marks, 0.0).astype(BF16)


def pick_marks(slots, ids):
    expert = iota((EXPERTS, ROWS), 0)
    named = jnp.zeros((EXPERTS, ROWS), F32)
    for k in range(ids.shape[0]):
        named = named + (ids[k : k + 1, :] == expert).astype(F32)
    return dot_t(slots, named)


def gates_of(logits, picks, me):
    sig = 1.0 / (1.0 + jnp.exp(-logits))
    total = jnp.sum(sig * picks, axis=1, keepdims=True)
    own = jnp.sum(jnp.where(iota(sig.shape, 1) == me, sig, 0.0), axis=1, keepdims=True)
    return jnp.where(total > 0.0, own / total, 0.0)


def silu(a):
    return a / (1.0 + jnp.exp(-a))


def start_all(pairs, sems):
    copies = []
    for k, (src, dst) in enumerate(pairs):
        copy = pltpu.make_async_copy(src, dst, sems.at[k])
        copy.start()
        copies.append(copy)
    return copies


def attend_kernel(
    len_hbm,
    q_hbm,
    new_hbm,
    ids_hbm,
    talk_hbm,
    kv_hbm,
    out_ref,
    chosen_ref,
    wanted_ref,
    picks_ref,
    place_ref,
    keep_ref,
    give_ref,
    len_ref,
    q_ref,
    new_ref,
    ids_ref,
    talk_ref,
    kv_ref,
    q_buf,
    o_buf,
    t_buf,
    sems,
):
    pairs = [(q_hbm, q_ref), (ids_hbm, ids_ref), (talk_hbm, talk_ref), (new_hbm, new_ref), (len_hbm, len_ref)]
    pairs += [(kv_hbm.at[t, c], kv_ref.at[t, c]) for t in range(2) for c in range(OWN)]
    copies = start_all(pairs, sems)
    small, keys, values = copies[:5], copies[5 : 5 + OWN], copies[5 + OWN :]
    for copy in small:
        copy.wait()
    seq = lax.axis_index("seq")
    scale = HD ** (-0.5)
    query = q_ref[...].astype(F32)
    for h in range(HEADS):
        q_buf[4 * h : 4 * h + 4, :] = query[:, HD * h : HD * h + HD]

    me = my_expert()
    group = lax.axis_index("exp")
    core = group & 1
    slots = slots_by_row(ids_ref[...], me)
    chosen_ref[...] = by_chunk(dot(slots, spread_marks(256, 2)), 4).astype(BF16)
    picks_ref[0] = pick_marks(slots, ids_ref[...])
    place_ref[...] = placing(slots, 128, 1)
    slots = slots_by_row(talk_ref[...], me)
    picks_ref[1] = pick_marks(slots, talk_ref[...])
    keep_ref[...] = placing(slots, 128, 2, core)
    give_ref[...] = placing(slots, 128, 2, 1 - core)
    slot = iota((8, ROWS), 0)
    own = jnp.logical_and(iota((8, ROWS), 1) == OWN * group + slot, slot < OWN)
    wanted = jnp.concatenate([slots, jnp.where(own, 1.0, 0.0)], axis=0)
    wanted_ref[...] = by_chunk(dot(wanted, spread_marks(128, 1)), 2).astype(BF16)

    lane = iota((HEADS, KVH * HD), 1)
    diag = (iota((HEADS, KVH * HD), 0) >> 3) == (lane >> 7)
    place = lane + seq * SPAN
    tail_lane = iota((HEADS, HD), 1)
    parts = []
    for c in range(OWN):
        q = q_buf[pl.ds(c, HEADS, stride=4), :]
        wide = jnp.where(diag, jnp.concatenate([q] * KVH, axis=1), 0.0)
        fresh_key = new_ref[0, c : c + 1, :].astype(F32)
        fresh = jnp.sum(wide * fresh_key, axis=1, keepdims=True) * scale
        parts.append((wide.astype(BF16), jnp.where(seq == 0, fresh, NEG)))
    for copy in keys:
        copy.wait()
    done = []
    for c in range(OWN):
        wide, fresh = parts[c]
        valid = place < len_ref[c]
        scores = jnp.where(valid, dot_t(wide, kv_ref[0, c]) * scale, NEG)
        peak = jnp.maximum(jnp.max(scores, axis=1, keepdims=True), fresh)
        peak = peak.astype(BF16).astype(F32)
        weights = jnp.where(valid, jnp.exp(scores - peak), 0.0).astype(BF16)
        fresh_weight = jnp.where(seq == 0, jnp.exp(fresh - peak), 0.0)
        total = jnp.sum(weights.astype(F32), axis=1, keepdims=True) + fresh_weight
        upper = total.astype(BF16).astype(F32)
        tail = jnp.where(tail_lane == 0, peak, jnp.where(tail_lane == 1, upper, total - upper))
        t_buf[pl.ds(c, HEADS, stride=4), :] = tail
        done.append((weights, fresh_weight))
    for copy in values:
        copy.wait()
    for c in range(OWN):
        weights, fresh_weight = done[c]
        fresh_value = new_ref[1, c : c + 1, :].astype(F32)
        mixed = dot(weights, kv_ref[1, c]) + fresh_weight * fresh_value
        mixed = jnp.where(diag, mixed, 0.0)
        mixed = (mixed[:, :HD] + mixed[:, HD : 2 * HD]) + (
            mixed[:, 2 * HD : 3 * HD] + mixed[:, 3 * HD :]
        )
        o_buf[pl.ds(c, HEADS, stride=4), :] = mixed
    out_ref[:, :, :HD] = o_buf[...].reshape(SEQ, 16, HD).astype(BF16)
    out_ref[:, :, HD:] = t_buf[...].reshape(SEQ, 16, HD).astype(BF16)


def project_kernel(recv_ref, proj_ref, out_ref, row_buf):
    got = recv_ref[...].astype(F32)
    peak = got[:, :, HD : HD + 1]
    total = got[:, :, HD + 1 : HD + 2] + got[:, :, HD + 2 : HD + 3]
    scale = jnp.exp(peak - jnp.max(peak, axis=0, keepdims=True))
    total = jnp.sum(scale * total, axis=0)
    mixed = jnp.sum(scale * got[:, :, :HD], axis=0) / total
    attn = jnp.concatenate([mixed[4 * h : 4 * h + 4] for h in range(4)], axis=1).astype(BF16)
    part = dot(attn, proj_ref[...])
    for j in range(4):
        row_buf[4 * j : 4 * j + 4, :] = part[:, 512 * j : 512 * j + 512]
    msg = row_buf[...].astype(BF16)
    for d in range(SEQ):
        out_ref[d] = msg


def norm_kernel(recv_ref, hidden_ref, gain_ref, out_ref, state_ref, buf, gain_buf):
    for j in range(4):
        cols = slice(512 * j, 512 * j + 512)
        buf[4 * j : 4 * j + 4, :] = hidden_ref[:, cols]
        gain_buf[4 * j : 4 * j + 4, :] = jnp.broadcast_to(gain_ref[:, cols], (OWN, 512))
    state = buf[...] + jnp.sum(recv_ref[...].astype(F32), axis=0)
    square = jnp.sum(state * state, axis=1, keepdims=True)
    square = (square[0:4] + square[4:8]) + (square[8:12] + square[12:16])
    inv = lax.rsqrt(square * (1.0 / D) + EPS)
    normed = (state * jnp.concatenate([inv] * 4, axis=0) * gain_buf[...]).astype(BF16)
    for d in range(EXP):
        out_ref[d] = normed
    buf[...] = state
    for s in range(SEQ):
        for k in range(2):
            first = (s % 2) * 256 + k * 128
            state_ref[s, 4 * k : 4 * k + 4, :] = buf[4 * (s // 2) : 4 * (s // 2) + 4, first : first + 128]


def expert_kernel(recv_ref, chosen_ref, picks_ref, place_ref, router_ref, up_ref, down_ref, out_ref):
    me = my_expert()
    rows = dot(chosen_ref[...], recv_ref[...])
    rows = jnp.concatenate([rows[8 * j : 8 * j + 8] for j in range(4)], axis=1).astype(BF16)
    gates = gates_of(dot(rows, router_ref[...]), picks_ref[0], me)
    both = dot(rows, up_ref[0])
    inner = (silu(both[:, :FF]) * both[:, FF:]).astype(BF16)
    reply = dot(inner, down_ref[0])
    reply = gates * reply.astype(BF16).astype(F32)
    halves = [
        jnp.concatenate(
            [reply[:, 256 * s + 128 * k : 256 * s + 128 * k + 128] for s in range(SEQ)], axis=1
        )
        for k in range(2)
    ]
    sent = dot(place_ref[...], jnp.concatenate(halves, axis=0).astype(BF16))
    for s in range(SEQ):
        block = sent[:, 128 * s : 128 * s + 128].reshape(EXP, 8, 128)
        out_ref[EXP * s : EXP * s + EXP] = block.astype(BF16)


def total_kernel(recv_ref, state_ref, out_ref):
    total = jnp.sum(recv_ref[...].astype(F32), axis=0) + state_ref[lax.axis_index("seq")]
    out_ref[...] = jnp.broadcast_to(total.astype(BF16)[None], out_ref.shape)


def talker_kernel(
    recv_ref,
    wanted_ref,
    picks_ref,
    keep_place_ref,
    give_place_ref,
    gain_ref,
    proj_ref,
    router_ref,
    up_ref,
    down_ref,
    thinker_ref,
    talk_ref,
    keep_ref,
    give_ref,
    row_buf,
    sem,
):
    me = my_expert()
    chosen = wanted_ref[...]
    parts = []
    for q in range(4):
        cols = []
        for s in (2 * q, 2 * q + 1):
            got = dot(chosen, recv_ref[128 * s : 128 * s + 128, :])
            cols += [got[:16], got[16:]]
        parts.append(jnp.concatenate(cols, axis=1))
        row_buf[:, 512 * q : 512 * q + 512] = parts[q][8 : 8 + OWN]
    out = pltpu.make_async_copy(row_buf, thinker_ref, sem)
    out.start()
    talk_in = jnp.zeros((16, DT), F32)
    for q in range(4):
        talk_in = talk_in + dot(parts[q].astype(BF16), proj_ref[512 * q : 512 * q + 512, :])
    talk_ref[...] = talk_in[8 : 8 + OWN]
    talk_in = talk_in[:8]
    mean = jnp.mean(talk_in * talk_in, axis=1, keepdims=True)
    normed = (talk_in * lax.rsqrt(mean + EPS) * gain_ref[...]).astype(BF16)
    gates = gates_of(dot(normed, router_ref[...]), picks_ref[1], me)
    both = dot(normed, up_ref[0])
    inner = (silu(both[:, :FT]) * both[:, FT:]).astype(BF16)
    reply = gates * dot(inner, down_ref[0]).astype(BF16).astype(F32)
    stacked = jnp.concatenate([reply[:, 256 * j : 256 * j + 256] for j in range(4)], axis=0)
    stacked = stacked.astype(BF16)
    keep_ref[...] = dot(keep_place_ref[...], stacked).reshape(8, 16, 256).astype(BF16)
    give_ref[...] = dot(give_place_ref[...], stacked).reshape(8, 16, 256).astype(BF16)
    out.wait()


def pair_kernel(keep_ref, got_ref, out_ref):
    total = (keep_ref[...].astype(F32) + got_ref[...].astype(F32)).astype(BF16)
    for s in range(SEQ):
        out_ref[8 * s : 8 * s + 8] = total


def finish_kernel(recv_ref, talk_ref, out_ref, buf):
    buf[...] = jnp.sum(recv_ref[...].astype(F32), axis=0)
    for j in range(4):
        cols = slice(256 * j, 256 * j + 256)
        out_ref[:, cols] = talk_ref[:, cols] + buf[4 * j : 4 * j + 4, :]


def call(kernel, outs, args, where, scratch=(), mib=16, flops=COST, outs_at=None):
    spaces = {"v": pltpu.VMEM, "s": pltpu.SMEM, "h": pltpu.HBM}
    many = isinstance(outs, list)
    whole = pl.BlockSpec(memory_space=pltpu.VMEM)
    return pl.pallas_call(
        kernel,
        out_shape=outs,
        in_specs=[pl.BlockSpec(memory_space=spaces[w]) for w in where],
        out_specs=[pl.BlockSpec(memory_space=spaces[w]) for w in outs_at or "v" * len(outs)] if many else whole,
        scratch_shapes=list(scratch),
        cost_estimate=pl.CostEstimate(flops=flops, bytes_accessed=1 << 20, transcendentals=0),
        compiler_params=pltpu.CompilerParams(vmem_limit_bytes=mib << 20),
    )(*args)


def array(shape, dtype):
    return jax.ShapeDtypeStruct(shape, dtype)


def exchange(msg, axis, groups=None):
    return lax.all_to_all(msg, axis, 0, 0, axis_index_groups=groups)


def on_device(
    queries,
    new_kv,
    kv_cache,
    lengths,
    out_proj,
    hidden_in,
    norm_gain,
    router,
    expert_ids,
    w_gate_up,
    w_down,
    talk_proj,
    talk_gain,
    talk_router,
    talk_ids,
    talk_gate_up,
    talk_down,
):
    both = ("seq", "exp")
    held = (lengths, queries, new_kv, expert_ids.T, talk_ids.T, kv_cache)
    msg, chosen, wanted, picks, place, keep_place, give_place = call(
        attend_kernel,
        [
            array((SEQ, 16, 256), BF16),
            array((32, 256), BF16),
            array((32, 128), BF16),
            array((2, 8, EXPERTS), F32),
            array((128, 16), BF16),
            array((128, 32), BF16),
            array((128, 32), BF16),
        ],
        tuple(pltpu.with_memory_space_constraint(x, pltpu.HBM) for x in held),
        "hhhhhh",
        [
            pltpu.SMEM((OWN,), jnp.int32),
            pltpu.VMEM((OWN, HEADS * HD), BF16),
            pltpu.VMEM((2, OWN, KVH * HD), BF16),
            pltpu.VMEM((8, ROWS), jnp.int32),
            pltpu.VMEM((8, ROWS), jnp.int32),
            pltpu.VMEM((2, OWN, SPAN, KVH * HD), BF16),
            pltpu.VMEM((HEADS * OWN, HD), F32),
            pltpu.VMEM((HEADS * OWN, HD), F32),
            pltpu.VMEM((HEADS * OWN, HD), F32),
            pltpu.SemaphoreType.DMA((5 + 2 * OWN,)),
        ],
    )
    msg = call(
        project_kernel,
        array((SEQ, 16, 512), BF16),
        (exchange(msg, "seq"), out_proj),
        "vv",
        [pltpu.VMEM((16, 512), F32)],
    )
    msg, state = call(
        norm_kernel,
        [array((EXP, 16, 512), BF16), array((SEQ, 8, 128), F32)],
        (exchange(msg, "seq"), hidden_in, norm_gain.reshape(1, D)),
        "vvv",
        [pltpu.VMEM((16, 512), F32), pltpu.VMEM((16, 512), F32)],
    )
    msg = call(
        expert_kernel,
        array((SEQ * EXP, 8, 128), BF16),
        (exchange(msg, "exp").reshape(256, 512), chosen, picks, place, router, w_gate_up, w_down),
        "vvvvvvv",
    )
    msg = call(
        total_kernel,
        array((SEQ * EXP, 8, 128), BF16),
        (exchange(msg, both), state),
        "vv",
    )
    thinker, talk_in, keep, give = call(
        talker_kernel,
        [
            array((OWN, D), F32),
            array((OWN, DT), F32),
            array((8, 16, 256), BF16),
            array((8, 16, 256), BF16),
        ],
        (
            exchange(msg, both).reshape(1024, 128),
            wanted,
            picks,
            keep_place,
            give_place,
            talk_gain.reshape(1, DT),
            talk_proj,
            talk_router,
            talk_gate_up,
            talk_down,
        ),
        "vvvvvvvvvv",
        [pltpu.VMEM((OWN, D), F32), pltpu.SemaphoreType.DMA],
        outs_at="hvvv",
    )
    got = lax.ppermute(give, "exp", [(e, e ^ 1) for e in range(EXP)])
    msg = call(pair_kernel, array((64, 16, 256), BF16), (keep, got), "vv")
    same_core = [[2 * i + core for i in range(64)] for core in range(2)]
    talker = call(
        finish_kernel,
        array((OWN, DT), F32),
        (exchange(msg, both, same_core), talk_in),
        "vv",
        [pltpu.VMEM((16, 256), F32)],
    )
    return (thinker, talker)


def solution(mesh):
    placed = (
        P("exp", None),
        P(None, "exp", None),
        P(None, "exp", "seq", None),
        P("exp"),
        P("seq", None),
        P("exp", None),
        P(),
        P(),
        P(),
        P(("seq", "exp"), None, None),
        P(("seq", "exp"), None, None),
        P(),
        P(),
        P(),
        P(),
        P(("seq", "exp"), None, None),
        P(("seq", "exp"), None, None),
    )
    return jax.shard_map(
        on_device,
        mesh=mesh,
        in_specs=placed,
        out_specs=(P("exp", None), P("exp", None)),
        check_vma=False,
    )
```

```python
import functools
import jax
import jax.numpy as jnp
from jax import lax
from jax.experimental import pallas as pl
from jax.experimental.pallas import tpu as pltpu
from jax.sharding import PartitionSpec as P

F32 = jnp.float32
BF16 = jnp.bfloat16
HEADS = 32
KVH = 4
HD = 128
D = 2048
DT = 1024
FF = 768
FT = 384
EXPERTS = 128
ROWS = 64
SEQ = 8
EXP = 16
OWN = 4
SPAN = 512
EPS = 1e-6
COST = 10**11
NEG = -1e30


def iota(shape, dim):
    return lax.broadcasted_iota(jnp.int32, shape, dim)


def dot(a, b):
    return jnp.dot(a, b, preferred_element_type=F32)


def dot_t(a, b):
    return lax.dot_general(a, b, (((1,), (1,)), ((), ())), preferred_element_type=F32)


def my_expert():
    return lax.axis_index("seq") * EXP + lax.axis_index("exp")


def slots_by_row(ids, me):
    match = jnp.sum((ids == me).astype(F32), axis=0, keepdims=True)
    match = jnp.broadcast_to(match, (8, ROWS))
    before = (iota((ROWS, ROWS), 0) < iota((ROWS, ROWS), 1)).astype(F32)
    rank = dot(match, before)
    hit = jnp.logical_and(rank == iota((8, ROWS), 0).astype(F32), match > 0.5)
    return jnp.where(hit, 1.0, 0.0)


def slots_of(ids, experts, slot):
    match = jnp.zeros(experts.shape, F32)
    for k in range(ids.shape[0]):
        match = match + (ids[k : k + 1, :] == experts).astype(F32)
    before = (iota((ROWS, ROWS), 0) < iota((ROWS, ROWS), 1)).astype(F32)
    rank = dot(match, before)
    hit = jnp.logical_and(rank == slot.astype(F32), match > 0.5)
    return jnp.where(hit, 1.0, 0.0)


def spread_marks(count, bits, group=None):
    r = iota((ROWS, count), 0)
    i = iota((ROWS, count), 1)
    owner = i >> (2 + bits)
    if group is not None:
        owner = 2 * owner + group
    same = jnp.logical_and(owner == (r >> 2), (i & 3) == (r & 3))
    return jnp.where(same, 1.0, 0.0)


def spread_marks_t(count, bits, group=None):
    i = iota((count, ROWS), 0)
    r = iota((count, ROWS), 1)
    owner = i >> (2 + bits)
    if group is not None:
        owner = 2 * owner + group
    same = jnp.logical_and(owner == (r >> 2), (i & 3) == (r & 3))
    return jnp.where(same, 1.0, 0.0)


def by_chunk(marks, chunks):
    i = iota(marks.shape, 1)
    return jnp.concatenate(
        [jnp.where(((i >> 2) & (chunks - 1)) == j, marks, 0.0) for j in range(chunks)], axis=0
    )


def placing(slots, count, bits, group=None):
    chunks = 1 << bits
    lanes = 8 * chunks
    marks = dot_t(spread_marks_t(count, bits, group), jnp.concatenate([slots] * chunks, axis=0))
    chunk = (iota((count, lanes), 0) >> 2) & (chunks - 1)
    return jnp.where((iota((count, lanes), 1) >> 3) == chunk, marks, 0.0).astype(BF16)


def pick_marks(slots, ids):
    expert = iota((EXPERTS, ROWS), 0)
    named = jnp.zeros((EXPERTS, ROWS), F32)
    for k in range(ids.shape[0]):
        named = named + (ids[k : k + 1, :] == expert).astype(F32)
    return dot_t(slots, named)


def gates_of(logits, picks, me):
    sig = 1.0 / (1.0 + jnp.exp(-logits))
    total = jnp.sum(sig * picks, axis=1, keepdims=True)
    own = jnp.sum(jnp.where(iota(sig.shape, 1) == me, sig, 0.0), axis=1, keepdims=True)
    return jnp.where(total > 0.0, own / total, 0.0)


def silu(a):
    return a / (1.0 + jnp.exp(-a))


def start_all(pairs, sems):
    copies = []
    for k, (src, dst) in enumerate(pairs):
        copy = pltpu.make_async_copy(src, dst, sems.at[k])
        copy.start()
        copies.append(copy)
    return copies


def attend_kernel(
    len_hbm,
    q_hbm,
    new_hbm,
    ids_hbm,
    talk_hbm,
    kv_hbm,
    out_ref,
    chosen_ref,
    picks_ref,
    sums_ref,
    carry_ref,
    state_ref,
    keep_ref,
    give_ref,
    first_ref,
    len_ref,
    q_ref,
    new_ref,
    ids_ref,
    talk_ref,
    kv_ref,
    q_buf,
    o_buf,
    t_buf,
    sems,
):
    pairs = [(q_hbm, q_ref), (ids_hbm, ids_ref), (talk_hbm, talk_ref), (new_hbm, new_ref), (len_hbm, len_ref)]
    pairs += [(kv_hbm.at[t, c], kv_ref.at[t, c]) for t in range(2) for c in range(OWN)]
    copies = start_all(pairs, sems)
    small, keys, values = copies[:5], copies[5 : 5 + OWN], copies[5 + OWN :]
    for copy in small:
        copy.wait()
    seq = lax.axis_index("seq")
    scale = HD ** (-0.5)
    query = q_ref[...].astype(F32)
    for h in range(HEADS):
        q_buf[4 * h : 4 * h + 4, :] = query[:, HD * h : HD * h + HD]

    me = my_expert()
    group = lax.axis_index("exp")
    core = group & 1
    ids = ids_ref[...]
    talk_ids = talk_ref[...]
    slots = slots_by_row(ids, me)
    chosen_ref[...] = by_chunk(dot(slots, spread_marks(256, 2)), 4).astype(BF16)
    picks_ref[0] = pick_marks(slots, ids)
    slots = slots_by_row(talk_ids, me)
    picks_ref[1] = pick_marks(slots, talk_ids)
    keep_ref[...] = placing(slots, 256, 3, core)
    give_ref[...] = placing(slots, 256, 3, 1 - core)
    first_ref[...] = dot_t(slots, jnp.broadcast_to((talk_ids[0:1, :] == me).astype(F32), (128, ROWS)))
    line = iota((128, ROWS), 0)
    came = slots_of(ids, (line >> 4) * EXP + group, line & 7)
    needed = slots_of(talk_ids, seq * EXP + (line >> 3), line & 7)
    half = (iota((128, 128), 1) >> 3) & 1
    sums = dot_t(needed, came)
    sums_ref[0] = jnp.where(half == 0, sums, 0.0).astype(BF16)
    sums_ref[1] = jnp.where(half == 1, sums, 0.0).astype(BF16)
    carry = dot_t(spread_marks_t(128, 1), came)
    carry_ref[...] = jnp.where(half == 1, carry, 0.0).astype(BF16)
    lane = iota((ROWS, 16), 1) - 8
    mine = jnp.logical_and(iota((ROWS, 16), 0) == OWN * group + lane, (lane >= 0) & (lane < OWN))
    state_ref[...] = dot(needed, jnp.where(mine, 1.0, 0.0)).astype(BF16)

    lane = iota((HEADS, KVH * HD), 1)
    diag = (iota((HEADS, KVH * HD), 0) >> 3) == (lane >> 7)
    place = lane + seq * SPAN
    tail_lane = iota((HEADS, HD), 1)
    parts = []
    for c in range(OWN):
        q = q_buf[pl.ds(c, HEADS, stride=4), :]
        wide = jnp.where(diag, jnp.concatenate([q] * KVH, axis=1), 0.0)
        fresh_key = new_ref[0, c : c + 1, :].astype(F32)
        fresh = jnp.sum(wide * fresh_key, axis=1, keepdims=True) * scale
        parts.append((wide.astype(BF16), jnp.where(seq == 0, fresh, NEG)))
    for copy in keys:
        copy.wait()
    done = []
    for c in range(OWN):
        wide, fresh = parts[c]
        valid = place < len_ref[c]
        scores = jnp.where(valid, dot_t(wide, kv_ref[0, c]) * scale, NEG)
        peak = jnp.maximum(jnp.max(scores, axis=1, keepdims=True), fresh)
        peak = peak.astype(BF16).astype(F32)
        weights = jnp.where(valid, jnp.exp(scores - peak), 0.0).astype(BF16)
        fresh_weight = jnp.where(seq == 0, jnp.exp(fresh - peak), 0.0)
        total = jnp.sum(weights.astype(F32), axis=1, keepdims=True) + fresh_weight
        upper = total.astype(BF16).astype(F32)
        tail = jnp.where(tail_lane == 0, peak, jnp.where(tail_lane == 1, upper, total - upper))
        t_buf[pl.ds(c, HEADS, stride=4), :] = tail
        done.append((weights, fresh_weight))
    for copy in values:
        copy.wait()
    for c in range(OWN):
        weights, fresh_weight = done[c]
        fresh_value = new_ref[1, c : c + 1, :].astype(F32)
        mixed = dot(weights, kv_ref[1, c]) + fresh_weight * fresh_value
        mixed = jnp.where(diag, mixed, 0.0)
        mixed = (mixed[:, :HD] + mixed[:, HD : 2 * HD]) + (
            mixed[:, 2 * HD : 3 * HD] + mixed[:, 3 * HD :]
        )
        o_buf[pl.ds(c, HEADS, stride=4), :] = mixed
    out_ref[:, :, :HD] = o_buf[...].reshape(SEQ, 16, HD).astype(BF16)
    out_ref[:, :, HD:] = t_buf[...].reshape(SEQ, 16, HD).astype(BF16)


def project_kernel(recv_ref, proj_ref, out_ref, row_buf):
    got = recv_ref[...].astype(F32)
    peak = got[:, :, HD : HD + 1]
    total = got[:, :, HD + 1 : HD + 2] + got[:, :, HD + 2 : HD + 3]
    scale = jnp.exp(peak - jnp.max(peak, axis=0, keepdims=True))
    total = jnp.sum(scale * total, axis=0)
    mixed = jnp.sum(scale * got[:, :, :HD], axis=0) / total
    attn = jnp.concatenate([mixed[4 * h : 4 * h + 4] for h in range(4)], axis=1).astype(BF16)
    part = dot(attn, proj_ref[...])
    for j in range(4):
        row_buf[4 * j : 4 * j + 4, :] = part[:, 512 * j : 512 * j + 512]
    msg = row_buf[...].astype(BF16)
    for d in range(SEQ):
        out_ref[d] = msg


def norm_kernel(recv_ref, hidden_ref, gain_ref, out_ref, state_ref, rows_ref, buf, gain_buf):
    for j in range(4):
        cols = slice(512 * j, 512 * j + 512)
        buf[4 * j : 4 * j + 4, :] = hidden_ref[:, cols]
        gain_buf[4 * j : 4 * j + 4, :] = jnp.broadcast_to(gain_ref[:, cols], (OWN, 512))
    state = buf[...] + jnp.sum(recv_ref[...].astype(F32), axis=0)
    square = jnp.sum(state * state, axis=1, keepdims=True)
    square = (square[0:4] + square[4:8]) + (square[8:12] + square[12:16])
    inv = lax.rsqrt(square * (1.0 / D) + EPS)
    normed = (state * jnp.concatenate([inv] * 4, axis=0) * gain_buf[...]).astype(BF16)
    for d in range(EXP):
        out_ref[d] = normed
    buf[...] = state
    for j in range(4):
        rows_ref[0:4, 512 * j : 512 * j + 512] = buf[4 * j : 4 * j + 4, :]
        rows_ref[4:8, 512 * j : 512 * j + 512] = jnp.zeros((4, 512), F32)
    for s in range(SEQ):
        for k in range(2):
            first = (s % 2) * 256 + k * 128
            state_ref[s, 4 * k : 4 * k + 4, :] = buf[4 * (s // 2) : 4 * (s // 2) + 4, first : first + 128]


def expert_kernel(
    recv_ref, chosen_ref, picks_ref, state_ref, router_ref, up_ref, down_ref, proj_ref, out_ref, mixed_ref
):
    me = my_expert()
    rows = dot(chosen_ref[...], recv_ref[...])
    rows = jnp.concatenate([rows[8 * j : 8 * j + 8] for j in range(4)], axis=1).astype(BF16)
    gates = gates_of(dot(rows, router_ref[...]), picks_ref[0], me)
    both = dot(rows, up_ref[0])
    inner = (silu(both[:, :FF]) * both[:, FF:]).astype(BF16)
    reply = dot(inner, down_ref[0])
    reply = gates * reply.astype(BF16).astype(F32)
    stacked = jnp.concatenate([reply, state_ref[...]], axis=0).astype(BF16)
    mixed = dot(stacked, proj_ref[...])
    mixed_ref[...] = mixed.astype(BF16)
    for s in range(SEQ):
        lower = jnp.concatenate([mixed[:8, 640:], reply[:, 256 * s : 256 * s + 256]], axis=1)
        out_ref[s] = jnp.concatenate([mixed[:8, :640], lower], axis=0).astype(BF16)


def route_kernel(recv_ref, sums_ref, carry_ref, state_mark_ref, mixed_ref, keep_ref, give_ref):
    upper = dot(sums_ref[0], recv_ref[...])
    lower = dot(sums_ref[1], recv_ref[:, :384])
    talk = jnp.concatenate([upper, lower], axis=1) + dot(state_mark_ref[...], mixed_ref[...])
    thinker = dot(carry_ref[...], recv_ref[:, 384:])
    odd = ((iota((128, 128), 0) >> 2) & 1) == 1
    thinker = jnp.where(odd, thinker[:, 128:], thinker[:, :128]).reshape(EXP, 8, 128)
    top = jnp.concatenate([talk[:, :512].reshape(EXP, 8, 512), thinker], axis=2)
    rest = jnp.concatenate([talk[:, 512:].reshape(EXP, 8, 512), jnp.zeros_like(thinker)], axis=2)
    msg = jnp.concatenate([top, rest], axis=1).astype(BF16).reshape(8, 2, 16, 640)
    first = (lax.axis_index("exp") & 1) == 0
    keep_ref[...] = jnp.where(first, msg[:, 0], msg[:, 1])
    give_ref[...] = jnp.where(first, msg[:, 1], msg[:, 0])


def join_kernel(keep_ref, got_ref, out_ref):
    out_ref[...] = (keep_ref[...].astype(F32) + got_ref[...].astype(F32)).astype(BF16)


def talker_kernel(
    recv_ref,
    state_ref,
    picks_ref,
    keep_place_ref,
    give_place_ref,
    first_ref,
    gain_ref,
    router_ref,
    up_ref,
    down_ref,
    thinker_ref,
    keep_ref,
    give_ref,
):
    me = my_expert()
    got = jnp.sum(recv_ref[...].astype(F32), axis=0)
    thinker_ref[...] = got[:8, 512:] + state_ref[lax.axis_index("seq")]
    talk_in = jnp.concatenate([got[:8, :512], got[8:, :512]], axis=1)
    mean = jnp.mean(talk_in * talk_in, axis=1, keepdims=True)
    normed = (talk_in * lax.rsqrt(mean + EPS) * gain_ref[...]).astype(BF16)
    gates = gates_of(dot(normed, router_ref[...]), picks_ref[1], me)
    both = dot(normed, up_ref[0])
    inner = (silu(both[:, :FT]) * both[:, FT:]).astype(BF16)
    reply = gates * dot(inner, down_ref[0]).astype(BF16).astype(F32)
    reply = reply + first_ref[:, :1] * talk_in
    stacked = jnp.concatenate([reply[:, 128 * j : 128 * j + 128] for j in range(8)], axis=0)
    stacked = stacked.astype(BF16)
    keep_ref[...] = dot(keep_place_ref[...], stacked).reshape(8, 32, 128).astype(BF16)
    give_ref[...] = dot(give_place_ref[...], stacked).reshape(8, 32, 128).astype(BF16)


def pair_kernel(keep_ref, got_ref, thinker_ref, out_ref):
    total = (keep_ref[...].astype(F32) + got_ref[...].astype(F32)).astype(BF16)
    thinker = jnp.broadcast_to(thinker_ref[...].astype(BF16)[None], (8, 8, 128))
    for s in range(SEQ):
        out_ref[8 * s : 8 * s + 8, :32, :] = total
        out_ref[8 * s : 8 * s + 8, 32:, :] = thinker


def finish_kernel(recv_ref, thinker_ref, out_ref, buf):
    buf[...] = jnp.sum(recv_ref[:, :32, :].astype(F32), axis=0)
    for j in range(8):
        out_ref[:, 128 * j : 128 * j + 128] = buf[4 * j : 4 * j + 4, :]
    pair = lax.axis_index("exp") >> 1
    for s in range(SEQ):
        block = recv_ref[8 * s + pair, 32:, :].astype(F32)
        for k in range(2):
            first = 256 * s + 128 * k
            thinker_ref[:, first : first + 128] = block[4 * k : 4 * k + 4]


def call(kernel, outs, args, where, scratch=(), mib=16, flops=COST, outs_at=None):
    spaces = {"v": pltpu.VMEM, "s": pltpu.SMEM, "h": pltpu.HBM}
    many = isinstance(outs, list)
    whole = pl.BlockSpec(memory_space=pltpu.VMEM)
    return pl.pallas_call(
        kernel,
        out_shape=outs,
        in_specs=[pl.BlockSpec(memory_space=spaces[w]) for w in where],
        out_specs=[pl.BlockSpec(memory_space=spaces[w]) for w in outs_at or "v" * len(outs)] if many else whole,
        scratch_shapes=list(scratch),
        cost_estimate=pl.CostEstimate(flops=flops, bytes_accessed=1 << 20, transcendentals=0),
        compiler_params=pltpu.CompilerParams(vmem_limit_bytes=mib << 20),
    )(*args)


def array(shape, dtype):
    return jax.ShapeDtypeStruct(shape, dtype)


SIDES = [[2 * i + core for i in range(8)] for core in range(2)]


def swap(msg):
    return lax.ppermute(msg, "exp", [(e, e ^ 1) for e in range(EXP)])


def exchange(msg, axis, groups=None):
    return lax.all_to_all(msg, axis, 0, 0, axis_index_groups=groups)


def on_device(
    queries,
    new_kv,
    kv_cache,
    lengths,
    out_proj,
    hidden_in,
    norm_gain,
    router,
    expert_ids,
    w_gate_up,
    w_down,
    talk_proj,
    talk_gain,
    talk_router,
    talk_ids,
    talk_gate_up,
    talk_down,
):
    both = ("seq", "exp")
    held = (lengths, queries, new_kv, expert_ids.T, talk_ids.T, kv_cache)
    msg, chosen, picks, sums, carry, state_mark, keep_place, give_place, first = call(
        attend_kernel,
        [
            array((SEQ, 16, 256), BF16),
            array((32, 256), BF16),
            array((2, 8, EXPERTS), F32),
            array((2, 128, 128), BF16),
            array((128, 128), BF16),
            array((128, 16), BF16),
            array((256, 64), BF16),
            array((256, 64), BF16),
            array((8, 128), F32),
        ],
        tuple(pltpu.with_memory_space_constraint(x, pltpu.HBM) for x in held),
        "hhhhhh",
        [
            pltpu.SMEM((OWN,), jnp.int32),
            pltpu.VMEM((OWN, HEADS * HD), BF16),
            pltpu.VMEM((2, OWN, KVH * HD), BF16),
            pltpu.VMEM((8, ROWS), jnp.int32),
            pltpu.VMEM((8, ROWS), jnp.int32),
            pltpu.VMEM((2, OWN, SPAN, KVH * HD), BF16),
            pltpu.VMEM((HEADS * OWN, HD), F32),
            pltpu.VMEM((HEADS * OWN, HD), F32),
            pltpu.VMEM((HEADS * OWN, HD), F32),
            pltpu.SemaphoreType.DMA((5 + 2 * OWN,)),
        ],
    )
    msg = call(
        project_kernel,
        array((SEQ, 16, 512), BF16),
        (exchange(msg, "seq"), out_proj),
        "vv",
        [pltpu.VMEM((16, 512), F32)],
    )
    msg, state, state_rows = call(
        norm_kernel,
        [array((EXP, 16, 512), BF16), array((SEQ, 8, 128), F32), array((8, D), F32)],
        (exchange(msg, "seq"), hidden_in, norm_gain.reshape(1, D)),
        "vvv",
        [pltpu.VMEM((16, 512), F32), pltpu.VMEM((16, 512), F32)],
    )
    msg, mixed = call(
        expert_kernel,
        [array((SEQ, 16, 640), BF16), array((16, DT), BF16)],
        (
            exchange(msg, "exp").reshape(256, 512),
            chosen,
            picks,
            state_rows,
            router,
            w_gate_up,
            w_down,
            talk_proj,
        ),
        "vvvvvvvv",
    )
    keep, give = call(
        route_kernel,
        [array((8, 16, 640), BF16), array((8, 16, 640), BF16)],
        (exchange(msg, "seq").reshape(128, 640), sums, carry, state_mark, mixed),
        "vvvvv",
    )
    got = swap(give)
    msg = call(join_kernel, array((8, 16, 640), BF16), (keep, got), "vv")
    block, keep, give = call(
        talker_kernel,
        [array((8, 128), F32), array((8, 32, 128), BF16), array((8, 32, 128), BF16)],
        (
            exchange(msg, "exp", SIDES),
            state,
            picks,
            keep_place,
            give_place,
            first,
            talk_gain.reshape(1, DT),
            talk_router,
            talk_gate_up,
            talk_down,
        ),
        "vvvvvvvvvv",
    )
    got = lax.ppermute(give, "exp", [(e, e ^ 1) for e in range(EXP)])
    msg = call(pair_kernel, array((64, 40, 128), BF16), (keep, got, block), "vvv")
    same_core = [[2 * i + core for i in range(64)] for core in range(2)]
    thinker, talker = call(
        finish_kernel,
        [array((OWN, D), F32), array((OWN, DT), F32)],
        (exchange(msg, both, same_core),),
        "v",
        [pltpu.VMEM((32, 128), F32)],
    )
    return (thinker, talker)


def solution(mesh):
    placed = (
        P("exp", None),
        P(None, "exp", None),
        P(None, "exp", "seq", None),
        P("exp"),
        P("seq", None),
        P("exp", None),
        P(),
        P(),
        P(),
        P(("seq", "exp"), None, None),
        P(("seq", "exp"), None, None),
        P(),
        P(),
        P(),
        P(),
        P(("seq", "exp"), None, None),
        P(("seq", "exp"), None, None),
    )
    return jax.shard_map(
        on_device,
        mesh=mesh,
        in_specs=placed,
        out_specs=(P("exp", None), P("exp", None)),
        check_vma=False,
    )
```

```python
import functools
import jax
import jax.numpy as jnp
from jax import lax
from jax.experimental import pallas as pl
from jax.experimental.pallas import tpu as pltpu
from jax.sharding import PartitionSpec as P

F32 = jnp.float32
BF16 = jnp.bfloat16
HEADS = 32
KVH = 4
HD = 128
D = 2048
DT = 1024
FF = 768
FT = 384
EXPERTS = 128
ROWS = 64
SEQ = 8
EXP = 16
OWN = 4
SPAN = 512
EPS = 1e-6
COST = 10**11
NEG = -1e30


def iota(shape, dim):
    return lax.broadcasted_iota(jnp.int32, shape, dim)


def dot(a, b):
    return jnp.dot(a, b, preferred_element_type=F32)


def dot_t(a, b):
    return lax.dot_general(a, b, (((1,), (1,)), ((), ())), preferred_element_type=F32)


def my_expert():
    return lax.axis_index("seq") * EXP + lax.axis_index("exp")


def expert_of(far, near):
    return (far & 7) * EXP + (far >> 3) * 8 + near


NEAR = [[expert_of(far, near) for near in range(8)] for far in range(16)]
FAR = [[expert_of(far, near) for far in range(16)] for near in range(8)]


def slots_by_row(ids, me):
    match = jnp.sum((ids == me).astype(F32), axis=0, keepdims=True)
    match = jnp.broadcast_to(match, (8, ROWS))
    before = (iota((ROWS, ROWS), 0) < iota((ROWS, ROWS), 1)).astype(F32)
    rank = dot(match, before)
    hit = jnp.logical_and(rank == iota((8, ROWS), 0).astype(F32), match > 0.5)
    return jnp.where(hit, 1.0, 0.0)


def slots_of(ids, experts, slot):
    match = jnp.zeros(experts.shape, F32)
    for k in range(ids.shape[0]):
        match = match + (ids[k : k + 1, :] == experts).astype(F32)
    before = (iota((ROWS, ROWS), 0) < iota((ROWS, ROWS), 1)).astype(F32)
    rank = dot(match, before)
    hit = jnp.logical_and(rank == slot.astype(F32), match > 0.5)
    return jnp.where(hit, 1.0, 0.0)


def spread_marks(count, bits):
    r = iota((ROWS, count), 0)
    i = iota((ROWS, count), 1)
    same = jnp.logical_and((i >> (2 + bits)) == (r >> 2), (i & 3) == (r & 3))
    return jnp.where(same, 1.0, 0.0)


def by_chunk(marks, chunks):
    i = iota(marks.shape, 1)
    return jnp.concatenate(
        [jnp.where(((i >> 2) & (chunks - 1)) == j, marks, 0.0) for j in range(chunks)], axis=0
    )


def pick_marks(slots, ids):
    expert = iota((EXPERTS, ROWS), 0)
    named = jnp.zeros((EXPERTS, ROWS), F32)
    for k in range(ids.shape[0]):
        named = named + (ids[k : k + 1, :] == expert).astype(F32)
    return dot_t(slots, named)


def gates_of(logits, picks, me):
    sig = 1.0 / (1.0 + jnp.exp(-logits))
    total = jnp.sum(sig * picks, axis=1, keepdims=True)
    own = jnp.sum(jnp.where(iota(sig.shape, 1) == me, sig, 0.0), axis=1, keepdims=True)
    return jnp.where(total > 0.0, own / total, 0.0)


def silu(a):
    return a / (1.0 + jnp.exp(-a))


def start_all(pairs, sems):
    copies = []
    for k, (src, dst) in enumerate(pairs):
        copy = pltpu.make_async_copy(src, dst, sems.at[k])
        copy.start()
        copies.append(copy)
    return copies


def attend_kernel(
    len_hbm,
    q_hbm,
    new_hbm,
    ids_hbm,
    talk_hbm,
    kv_hbm,
    out_ref,
    chosen_ref,
    picks_ref,
    sums_ref,
    carry_ref,
    place_ref,
    first_ref,
    len_ref,
    q_ref,
    new_ref,
    ids_ref,
    talk_ref,
    kv_ref,
    q_buf,
    o_buf,
    t_buf,
    sems,
):
    pairs = [(q_hbm, q_ref), (ids_hbm, ids_ref), (talk_hbm, talk_ref), (new_hbm, new_ref), (len_hbm, len_ref)]
    pairs += [(kv_hbm.at[t, c], kv_ref.at[t, c]) for t in range(2) for c in range(OWN)]
    copies = start_all(pairs, sems)
    small, keys, values = copies[:5], copies[5 : 5 + OWN], copies[5 + OWN :]
    for copy in small:
        copy.wait()
    seq = lax.axis_index("seq")
    scale = HD ** (-0.5)
    query = q_ref[...].astype(F32)
    for h in range(HEADS):
        q_buf[4 * h : 4 * h + 4, :] = query[:, HD * h : HD * h + HD]

    me = my_expert()
    near = lax.axis_index("exp") & 7
    far = (lax.axis_index("exp") >> 3) * 8 + seq
    ids = ids_ref[...]
    talk_ids = talk_ref[...]
    slots = slots_by_row(ids, me)
    talk_slots = slots_by_row(talk_ids, me)
    picks_ref[0] = pick_marks(slots, ids)
    picks_ref[1] = pick_marks(talk_slots, talk_ids)
    both = jnp.concatenate([slots, talk_slots], axis=0)
    chosen_ref[...] = by_chunk(dot(both, spread_marks(256, 2)), 4).astype(BF16)
    first = (talk_ids[0:1, :] == me).astype(F32)
    first_ref[...] = dot_t(talk_slots, jnp.broadcast_to(first, (128, ROWS)))
    line = iota((128, ROWS), 0)
    came = slots_of(ids, expert_of(far, line >> 4), line & 7)
    needed = slots_of(talk_ids, expert_of(line >> 3, near), line & 7)
    half = (iota((128, 128), 1) >> 3) & 1
    sums = dot_t(needed, came)
    sums_ref[0] = jnp.where(half == 0, sums, 0.0).astype(BF16)
    sums_ref[1] = jnp.where(half == 1, sums, 0.0).astype(BF16)
    line = iota((ROWS, ROWS), 0)
    row = ((line >> 2) & 1) * 32 + (line >> 3) * 4 + (line & 3)
    turn = jnp.where(row == iota((ROWS, ROWS), 1), 1.0, 0.0)
    line = iota((128, ROWS), 0)
    carry_ref[...] = dot_t(turn, slots_of(ids, expert_of(line >> 3, near), line & 7)).astype(BF16)
    place_ref[...] = dot_t(turn, jnp.concatenate([talk_slots, jnp.zeros_like(talk_slots)], axis=0)).astype(BF16)

    lane = iota((HEADS, KVH * HD), 1)
    diag = (iota((HEADS, KVH * HD), 0) >> 3) == (lane >> 7)
    place = lane + seq * SPAN
    tail_lane = iota((HEADS, HD), 1)
    parts = []
    for c in range(OWN):
        q = q_buf[pl.ds(c, HEADS, stride=4), :]
        wide = jnp.where(diag, jnp.concatenate([q] * KVH, axis=1), 0.0)
        fresh_key = new_ref[0, c : c + 1, :].astype(F32)
        fresh = jnp.sum(wide * fresh_key, axis=1, keepdims=True) * scale
        parts.append((wide.astype(BF16), jnp.where(seq == 0, fresh, NEG)))
    for copy in keys:
        copy.wait()
    done = []
    for c in range(OWN):
        wide, fresh = parts[c]
        valid = place < len_ref[c]
        scores = jnp.where(valid, dot_t(wide, kv_ref[0, c]) * scale, NEG)
        peak = jnp.maximum(jnp.max(scores, axis=1, keepdims=True), fresh)
        peak = peak.astype(BF16).astype(F32)
        weights = jnp.where(valid, jnp.exp(scores - peak), 0.0).astype(BF16)
        fresh_weight = jnp.where(seq == 0, jnp.exp(fresh - peak), 0.0)
        total = jnp.sum(weights.astype(F32), axis=1, keepdims=True) + fresh_weight
        upper = total.astype(BF16).astype(F32)
        tail = jnp.where(tail_lane == 0, peak, jnp.where(tail_lane == 1, upper, total - upper))
        t_buf[pl.ds(c, HEADS, stride=4), :] = tail
        done.append((weights, fresh_weight))
    for copy in values:
        copy.wait()
    for c in range(OWN):
        weights, fresh_weight = done[c]
        fresh_value = new_ref[1, c : c + 1, :].astype(F32)
        mixed = dot(weights, kv_ref[1, c]) + fresh_weight * fresh_value
        mixed = jnp.where(diag, mixed, 0.0)
        mixed = (mixed[:, :HD] + mixed[:, HD : 2 * HD]) + (
            mixed[:, 2 * HD : 3 * HD] + mixed[:, 3 * HD :]
        )
        o_buf[pl.ds(c, HEADS, stride=4), :] = mixed
    out_ref[:, :, :HD] = o_buf[...].reshape(SEQ, 16, HD).astype(BF16)
    out_ref[:, :, HD:] = t_buf[...].reshape(SEQ, 16, HD).astype(BF16)


def project_kernel(recv_ref, proj_ref, out_ref, row_buf):
    got = recv_ref[...].astype(F32)
    peak = got[:, :, HD : HD + 1]
    total = got[:, :, HD + 1 : HD + 2] + got[:, :, HD + 2 : HD + 3]
    scale = jnp.exp(peak - jnp.max(peak, axis=0, keepdims=True))
    total = jnp.sum(scale * total, axis=0)
    mixed = jnp.sum(scale * got[:, :, :HD], axis=0) / total
    attn = jnp.concatenate([mixed[4 * h : 4 * h + 4] for h in range(4)], axis=1).astype(BF16)
    part = dot(attn, proj_ref[...])
    for j in range(4):
        row_buf[4 * j : 4 * j + 4, :] = part[:, 512 * j : 512 * j + 512]
    msg = row_buf[...].astype(BF16)
    for d in range(SEQ):
        out_ref[d] = msg


def state_kernel(recv_ref, hidden_ref, out_ref, rows_ref, buf):
    for j in range(4):
        buf[4 * j : 4 * j + 4, :] = hidden_ref[:, 512 * j : 512 * j + 512]
    buf[...] = buf[...] + jnp.sum(recv_ref[...].astype(F32), axis=0)
    msg = buf[...].astype(BF16)
    for d in range(EXP):
        out_ref[d] = msg
    for j in range(4):
        rows_ref[:, 512 * j : 512 * j + 512] = buf[4 * j : 4 * j + 4, :]


def normed(stream, gain):
    mean = jnp.mean(stream * stream, axis=1, keepdims=True)
    return (stream * lax.rsqrt(mean + EPS) * gain).astype(BF16)


def expert_kernel(
    recv_ref,
    chosen_ref,
    picks_ref,
    gain_ref,
    router_ref,
    up_ref,
    down_ref,
    proj_ref,
    out_ref,
    reply_ref,
    talk_ref,
):
    me = my_expert()
    rows = dot(chosen_ref[...], recv_ref[...])
    rows = jnp.concatenate([rows[16 * j : 16 * j + 16] for j in range(4)], axis=1)
    own = normed(rows[:8], gain_ref[...])
    gates = gates_of(dot(own, router_ref[...]), picks_ref[0], me)
    both = dot(own, up_ref[0])
    inner = (silu(both[:, :FF]) * both[:, FF:]).astype(BF16)
    reply = dot(inner, down_ref[0])
    reply = gates * reply.astype(BF16).astype(F32)
    mixed = dot(jnp.concatenate([reply, rows[8:]], axis=0).astype(BF16), proj_ref[...])
    talk_ref[...] = mixed[8:]
    msg = jnp.concatenate([mixed[:8, :512], mixed[:8, 512:]], axis=0).astype(BF16)
    for d in range(8):
        out_ref[d] = msg
    for d in range(16):
        reply_ref[d] = reply[:, 128 * d : 128 * d + 128]


def route_kernel(recv_ref, sums_ref, reply_ref, out_ref):
    upper = dot(sums_ref[0], recv_ref[...])
    lower = dot(sums_ref[1], recv_ref[...])
    talk = [upper[:, 128 * k : 128 * k + 128].reshape(16, 8, 128) for k in range(4)]
    talk += [lower[:, 128 * k : 128 * k + 128].reshape(16, 8, 128) for k in range(4)]
    out_ref[...] = jnp.concatenate(talk + [reply_ref[...]], axis=1).astype(BF16)


def talker_kernel(
    recv_ref,
    talk_ref,
    picks_ref,
    carry_ref,
    place_ref,
    first_ref,
    gain_ref,
    router_ref,
    up_ref,
    down_ref,
    out_ref,
):
    me = my_expert()
    got = jnp.sum(recv_ref[:, :64, :].astype(F32), axis=0)
    talk_in = jnp.concatenate([got[8 * k : 8 * k + 8] for k in range(8)], axis=1) + talk_ref[...]
    own = normed(talk_in, gain_ref[...])
    gates = gates_of(dot(own, router_ref[...]), picks_ref[1], me)
    both = dot(own, up_ref[0])
    inner = (silu(both[:, :FT]) * both[:, FT:]).astype(BF16)
    reply = gates * dot(inner, down_ref[0]).astype(BF16).astype(F32)
    reply = reply + first_ref[:, :1] * talk_in
    reply = jnp.concatenate([reply, jnp.zeros_like(reply)], axis=0).astype(BF16)
    sent = dot(place_ref[...], reply)
    sent = [sent[:, 128 * k : 128 * k + 128].reshape(8, 8, 128) for k in range(8)]
    came = recv_ref[:, 64:, :].astype(F32).reshape(128, 128).astype(BF16)
    thinker = dot(carry_ref[...], came).reshape(8, 8, 128)
    out_ref[...] = jnp.concatenate(sent + [thinker], axis=1).astype(BF16)


def pass_kernel(recv_ref, out_ref, got_buf, buf):
    got_buf[...] = jnp.sum(recv_ref[...].astype(F32), axis=0)
    for side in range(2):
        for k in range(9):
            buf[side, 4 * k : 4 * k + 4, :] = got_buf[8 * k + 4 * side : 8 * k + 4 * side + 4, :]
        buf[side, 36:, :] = jnp.zeros((4, 128), F32)
    for d in range(16):
        out_ref[d] = buf[d >> 3].astype(BF16)


def finish_kernel(recv_ref, state_ref, thinker_ref, out_ref, buf):
    buf[...] = jnp.sum(recv_ref[:, :32, :].astype(F32), axis=0)
    for k in range(8):
        out_ref[:, 128 * k : 128 * k + 128] = buf[4 * k : 4 * k + 4, :]
    for d in range(16):
        cols = slice(128 * d, 128 * d + 128)
        thinker_ref[:, cols] = state_ref[:, cols] + recv_ref[d, 32:, :].astype(F32)[:OWN]


def call(kernel, outs, args, where, scratch=(), mib=16, flops=COST, outs_at=None):
    spaces = {"v": pltpu.VMEM, "s": pltpu.SMEM, "h": pltpu.HBM}
    many = isinstance(outs, list)
    whole = pl.BlockSpec(memory_space=pltpu.VMEM)
    return pl.pallas_call(
        kernel,
        out_shape=outs,
        in_specs=[pl.BlockSpec(memory_space=spaces[w]) for w in where],
        out_specs=[pl.BlockSpec(memory_space=spaces[w]) for w in outs_at or "v" * len(outs)] if many else whole,
        scratch_shapes=list(scratch),
        cost_estimate=pl.CostEstimate(flops=flops, bytes_accessed=1 << 20, transcendentals=0),
        compiler_params=pltpu.CompilerParams(vmem_limit_bytes=mib << 20),
    )(*args)


def array(shape, dtype):
    return jax.ShapeDtypeStruct(shape, dtype)


def exchange(msg, axis, groups=None):
    return lax.all_to_all(msg, axis, 0, 0, axis_index_groups=groups)


def on_device(
    queries,
    new_kv,
    kv_cache,
    lengths,
    out_proj,
    hidden_in,
    norm_gain,
    router,
    expert_ids,
    w_gate_up,
    w_down,
    talk_proj,
    talk_gain,
    talk_router,
    talk_ids,
    talk_gate_up,
    talk_down,
):
    both = ("seq", "exp")
    held = (lengths, queries, new_kv, expert_ids.T, talk_ids.T, kv_cache)
    msg, chosen, picks, sums, carry, place, first = call(
        attend_kernel,
        [
            array((SEQ, 16, 256), BF16),
            array((64, 256), BF16),
            array((2, 8, EXPERTS), F32),
            array((2, 128, 128), BF16),
            array((64, 128), BF16),
            array((64, 16), BF16),
            array((8, 128), F32),
        ],
        tuple(pltpu.with_memory_space_constraint(x, pltpu.HBM) for x in held),
        "hhhhhh",
        [
            pltpu.SMEM((OWN,), jnp.int32),
            pltpu.VMEM((OWN, HEADS * HD), BF16),
            pltpu.VMEM((2, OWN, KVH * HD), BF16),
            pltpu.VMEM((8, ROWS), jnp.int32),
            pltpu.VMEM((8, ROWS), jnp.int32),
            pltpu.VMEM((2, OWN, SPAN, KVH * HD), BF16),
            pltpu.VMEM((HEADS * OWN, HD), F32),
            pltpu.VMEM((HEADS * OWN, HD), F32),
            pltpu.VMEM((HEADS * OWN, HD), F32),
            pltpu.SemaphoreType.DMA((5 + 2 * OWN,)),
        ],
    )
    msg = call(
        project_kernel,
        array((SEQ, 16, 512), BF16),
        (exchange(msg, "seq"), out_proj),
        "vv",
        [pltpu.VMEM((16, 512), F32)],
    )
    msg, state = call(
        state_kernel,
        [array((EXP, 16, 512), BF16), array((OWN, D), F32)],
        (exchange(msg, "seq"), hidden_in),
        "vv",
        [pltpu.VMEM((16, 512), F32)],
    )
    msg, reply, talk_in = call(
        expert_kernel,
        [array((8, 16, 512), BF16), array((16, 8, 128), F32), array((8, DT), F32)],
        (
            exchange(msg, "exp").reshape(256, 512),
            chosen,
            picks,
            norm_gain.reshape(1, D),
            router,
            w_gate_up,
            w_down,
            talk_proj,
        ),
        "vvvvvvvv",
    )
    msg = call(
        route_kernel,
        array((16, 72, 128), BF16),
        (exchange(msg, both, NEAR).reshape(128, 512), sums, reply),
        "vvv",
    )
    msg = call(
        talker_kernel,
        array((8, 72, 128), BF16),
        (
            exchange(msg, both, FAR),
            talk_in,
            picks,
            carry,
            place,
            first,
            talk_gain.reshape(1, DT),
            talk_router,
            talk_gate_up,
            talk_down,
        ),
        "vvvvvvvvvv",
    )
    msg = call(
        pass_kernel,
        array((16, 40, 128), BF16),
        (exchange(msg, both, NEAR),),
        "v",
        [pltpu.VMEM((72, 128), F32), pltpu.VMEM((2, 40, 128), F32)],
    )
    thinker, talker = call(
        finish_kernel,
        [array((OWN, D), F32), array((OWN, DT), F32)],
        (exchange(msg, both, FAR), state),
        "vv",
        [pltpu.VMEM((32, 128), F32)],
    )
    return (thinker, talker)


def solution(mesh):
    placed = (
        P("exp", None),
        P(None, "exp", None),
        P(None, "exp", "seq", None),
        P("exp"),
        P("seq", None),
        P("exp", None),
        P(),
        P(),
        P(),
        P(("seq", "exp"), None, None),
        P(("seq", "exp"), None, None),
        P(),
        P(),
        P(),
        P(),
        P(("seq", "exp"), None, None),
        P(("seq", "exp"), None, None),
    )
    return jax.shard_map(
        on_device,
        mesh=mesh,
        in_specs=placed,
        out_specs=(P("exp", None), P("exp", None)),
        check_vma=False,
    )
```

```python
import functools
import jax
import jax.numpy as jnp
from jax import lax
from jax.experimental import pallas as pl
from jax.experimental.pallas import tpu as pltpu
from jax.sharding import PartitionSpec as P

F32 = jnp.float32
BF16 = jnp.bfloat16
HEADS = 32
KVH = 4
HD = 128
D = 2048
DT = 1024
FF = 768
FT = 384
EXPERTS = 128
ROWS = 64
SEQ = 8
EXP = 16
OWN = 4
SPAN = 512
EPS = 1e-6
COST = 10**11
NEG = -1e30


def iota(shape, dim):
    return lax.broadcasted_iota(jnp.int32, shape, dim)


def dot(a, b):
    return jnp.dot(a, b, preferred_element_type=F32)


def dot_t(a, b):
    return lax.dot_general(a, b, (((1,), (1,)), ((), ())), preferred_element_type=F32)


def my_expert():
    return lax.axis_index("seq") * EXP + lax.axis_index("exp")


def expert_of(far, near):
    return (far & 7) * EXP + (far >> 3) * 8 + near


NEAR = [[expert_of(far, near) for near in range(8)] for far in range(16)]
FAR = [[expert_of(far, near) for far in range(16)] for near in range(8)]


def slots_by_row(ids, me):
    match = jnp.sum((ids == me).astype(F32), axis=0, keepdims=True)
    match = jnp.broadcast_to(match, (8, ROWS))
    before = (iota((ROWS, ROWS), 0) < iota((ROWS, ROWS), 1)).astype(F32)
    rank = dot(match, before)
    hit = jnp.logical_and(rank == iota((8, ROWS), 0).astype(F32), match > 0.5)
    return jnp.where(hit, 1.0, 0.0)


def slots_of(ids, experts, slot):
    match = jnp.zeros(experts.shape, F32)
    for k in range(ids.shape[0]):
        match = match + (ids[k : k + 1, :] == experts).astype(F32)
    before = (iota((ROWS, ROWS), 0) < iota((ROWS, ROWS), 1)).astype(F32)
    rank = dot(match, before)
    hit = jnp.logical_and(rank == slot.astype(F32), match > 0.5)
    return jnp.where(hit, 1.0, 0.0)


def spread_marks(count, bits):
    r = iota((ROWS, count), 0)
    i = iota((ROWS, count), 1)
    same = jnp.logical_and((i >> (2 + bits)) == (r >> 2), (i & 3) == (r & 3))
    return jnp.where(same, 1.0, 0.0)


def by_chunk(marks, chunks):
    i = iota(marks.shape, 1)
    return jnp.concatenate(
        [jnp.where(((i >> 2) & (chunks - 1)) == j, marks, 0.0) for j in range(chunks)], axis=0
    )


def pick_marks(slots, ids):
    expert = iota((EXPERTS, ROWS), 0)
    named = jnp.zeros((EXPERTS, ROWS), F32)
    for k in range(ids.shape[0]):
        named = named + (ids[k : k + 1, :] == expert).astype(F32)
    return dot_t(slots, named)


def gates_of(logits, picks, me):
    sig = 1.0 / (1.0 + jnp.exp(-logits))
    total = jnp.sum(sig * picks, axis=1, keepdims=True)
    own = jnp.sum(jnp.where(iota(sig.shape, 1) == me, sig, 0.0), axis=1, keepdims=True)
    return jnp.where(total > 0.0, own / total, 0.0)


def silu(a):
    return a / (1.0 + jnp.exp(-a))


def start_all(pairs, sems):
    copies = []
    for k, (src, dst) in enumerate(pairs):
        copy = pltpu.make_async_copy(src, dst, sems.at[k])
        copy.start()
        copies.append(copy)
    return copies


def attend_kernel(
    len_hbm,
    q_hbm,
    new_hbm,
    ids_hbm,
    talk_hbm,
    kv_hbm,
    out_ref,
    chosen_ref,
    picks_ref,
    sums_ref,
    carry_ref,
    place_ref,
    first_ref,
    len_ref,
    q_ref,
    new_ref,
    ids_ref,
    talk_ref,
    kv_ref,
    q_buf,
    o_buf,
    t_buf,
    sems,
):
    pairs = [(q_hbm, q_ref), (ids_hbm, ids_ref), (talk_hbm, talk_ref), (new_hbm, new_ref), (len_hbm, len_ref)]
    pairs += [(kv_hbm.at[t, c], kv_ref.at[t, c]) for t in range(2) for c in range(OWN)]
    copies = start_all(pairs, sems)
    small, keys, values = copies[:5], copies[5 : 5 + OWN], copies[5 + OWN :]
    for copy in small:
        copy.wait()
    seq = lax.axis_index("seq")
    scale = HD ** (-0.5)
    query = q_ref[...].astype(F32)
    for h in range(HEADS):
        q_buf[4 * h : 4 * h + 4, :] = query[:, HD * h : HD * h + HD]

    me = my_expert()
    near = lax.axis_index("exp") & 7
    far = (lax.axis_index("exp") >> 3) * 8 + seq
    ids = ids_ref[...]
    talk_ids = talk_ref[...]
    slots = slots_by_row(ids, me)
    talk_slots = slots_by_row(talk_ids, me)
    picks_ref[0] = pick_marks(slots, ids)
    picks_ref[1] = pick_marks(talk_slots, talk_ids)
    both = jnp.concatenate([slots, talk_slots], axis=0)
    chosen_ref[...] = by_chunk(dot(both, spread_marks(256, 2)), 4).astype(BF16)
    first = (talk_ids[0:1, :] == me).astype(F32)
    first_ref[...] = dot_t(talk_slots, jnp.broadcast_to(first, (128, ROWS)))
    line = iota((128, ROWS), 0)
    came = slots_of(ids, expert_of(far, line >> 4), line & 7)
    needed = slots_of(talk_ids, expert_of(line >> 3, near), line & 7)
    half = (iota((128, 128), 1) >> 3) & 1
    sums = dot_t(needed, came)
    sums_ref[0] = jnp.where(half == 0, sums, 0.0).astype(BF16)
    sums_ref[1] = jnp.where(half == 1, sums, 0.0).astype(BF16)
    line = iota((ROWS, ROWS), 0)
    row = ((line >> 2) & 1) * 32 + (line >> 3) * 4 + (line & 3)
    turn = jnp.where(row == iota((ROWS, ROWS), 1), 1.0, 0.0)
    line = iota((128, ROWS), 0)
    carry_ref[...] = dot_t(turn, slots_of(ids, expert_of(line >> 3, near), line & 7)).astype(BF16)
    place_ref[...] = dot_t(turn, jnp.concatenate([talk_slots, jnp.zeros_like(talk_slots)], axis=0)).astype(BF16)

    lane = iota((HEADS, KVH * HD), 1)
    diag = (iota((HEADS, KVH * HD), 0) >> 3) == (lane >> 7)
    place = lane + seq * SPAN
    tail_lane = iota((HEADS, HD), 1)
    parts = []
    for c in range(OWN):
        q = q_buf[pl.ds(c, HEADS, stride=4), :]
        wide = jnp.where(diag, jnp.concatenate([q] * KVH, axis=1), 0.0)
        fresh_key = new_ref[0, c : c + 1, :].astype(F32)
        fresh = jnp.sum(wide * fresh_key, axis=1, keepdims=True) * scale
        parts.append((wide.astype(BF16), jnp.where(seq == 0, fresh, NEG)))
    for copy in keys:
        copy.wait()
    done = []
    for c in range(OWN):
        wide, fresh = parts[c]
        valid = place < len_ref[c]
        scores = jnp.where(valid, dot_t(wide, kv_ref[0, c]) * scale, NEG)
        peak = jnp.maximum(jnp.max(scores, axis=1, keepdims=True), fresh)
        peak = peak.astype(BF16).astype(F32)
        weights = jnp.where(valid, jnp.exp(scores - peak), 0.0).astype(BF16)
        fresh_weight = jnp.where(seq == 0, jnp.exp(fresh - peak), 0.0)
        total = jnp.sum(weights.astype(F32), axis=1, keepdims=True) + fresh_weight
        upper = total.astype(BF16).astype(F32)
        tail = jnp.where(tail_lane == 0, peak, jnp.where(tail_lane == 1, upper, total - upper))
        t_buf[pl.ds(c, HEADS, stride=4), :] = tail
        done.append((weights, fresh_weight))
    for copy in values:
        copy.wait()
    for c in range(OWN):
        weights, fresh_weight = done[c]
        fresh_value = new_ref[1, c : c + 1, :].astype(F32)
        mixed = dot(weights, kv_ref[1, c]) + fresh_weight * fresh_value
        mixed = jnp.where(diag, mixed, 0.0)
        mixed = (mixed[:, :HD] + mixed[:, HD : 2 * HD]) + (
            mixed[:, 2 * HD : 3 * HD] + mixed[:, 3 * HD :]
        )
        o_buf[pl.ds(c, HEADS, stride=4), :] = mixed
    out_ref[:, :, :HD] = o_buf[...].reshape(SEQ, 16, HD).astype(BF16)
    out_ref[:, :, HD:] = t_buf[...].reshape(SEQ, 16, HD).astype(BF16)


def project_kernel(recv_ref, proj_ref, out_ref, row_buf):
    got = recv_ref[...].astype(F32)
    peak = got[:, :, HD : HD + 1]
    total = got[:, :, HD + 1 : HD + 2] + got[:, :, HD + 2 : HD + 3]
    scale = jnp.exp(peak - jnp.max(peak, axis=0, keepdims=True))
    total = jnp.sum(scale * total, axis=0)
    mixed = jnp.sum(scale * got[:, :, :HD], axis=0) / total
    attn = jnp.concatenate([mixed[4 * h : 4 * h + 4] for h in range(4)], axis=1).astype(BF16)
    part = dot(attn, proj_ref[...])
    for j in range(4):
        row_buf[4 * j : 4 * j + 4, :] = part[:, 512 * j : 512 * j + 512]
    msg = row_buf[...].astype(BF16)
    for d in range(SEQ):
        out_ref[d] = msg


def state_kernel(recv_ref, hidden_ref, out_ref, rows_ref, buf):
    for j in range(4):
        buf[4 * j : 4 * j + 4, :] = hidden_ref[:, 512 * j : 512 * j + 512]
    buf[...] = buf[...] + jnp.sum(recv_ref[...].astype(F32), axis=0)
    msg = buf[...].astype(BF16)
    for d in range(EXP):
        out_ref[d] = msg
    for j in range(4):
        rows_ref[:, 512 * j : 512 * j + 512] = buf[4 * j : 4 * j + 4, :]


def inverse(stream):
    return lax.rsqrt(jnp.mean(stream * stream, axis=1, keepdims=True) + EPS)


def expert_kernel(
    recv_ref,
    chosen_ref,
    picks_ref,
    gain_ref,
    router_ref,
    up_ref,
    down_ref,
    proj_ref,
    out_ref,
    reply_ref,
    talk_ref,
):
    me = my_expert()
    rows = dot(chosen_ref[...], recv_ref[...])
    rows = jnp.concatenate([rows[16 * j : 16 * j + 16] for j in range(4)], axis=1)
    inv = inverse(rows[:8])
    own = (rows[:8] * gain_ref[...]).astype(BF16)
    gates = gates_of(dot(own, router_ref[...]) * inv, picks_ref[0], me)
    both = dot(own, up_ref[0]) * inv
    inner = (silu(both[:, :FF]) * both[:, FF:]).astype(BF16)
    reply = dot(inner, down_ref[0])
    reply = gates * reply.astype(BF16).astype(F32)
    mixed = dot(jnp.concatenate([reply, rows[8:]], axis=0).astype(BF16), proj_ref[...])
    talk_ref[...] = mixed[8:]
    msg = jnp.concatenate([mixed[:8, :512], mixed[:8, 512:]], axis=0).astype(BF16)
    for d in range(8):
        out_ref[d] = msg
    for d in range(16):
        reply_ref[d] = reply[:, 128 * d : 128 * d + 128]


def route_kernel(recv_ref, sums_ref, reply_ref, out_ref):
    upper = dot(sums_ref[0], recv_ref[...])
    lower = dot(sums_ref[1], recv_ref[...])
    talk = [upper[:, 128 * k : 128 * k + 128].reshape(16, 8, 128) for k in range(4)]
    talk += [lower[:, 128 * k : 128 * k + 128].reshape(16, 8, 128) for k in range(4)]
    out_ref[...] = jnp.concatenate(talk + [reply_ref[...]], axis=1).astype(BF16)


def talker_kernel(
    recv_ref,
    talk_ref,
    picks_ref,
    carry_ref,
    place_ref,
    first_ref,
    gain_ref,
    router_ref,
    up_ref,
    down_ref,
    out_ref,
):
    me = my_expert()
    got = jnp.sum(recv_ref[:, :64, :].astype(F32), axis=0)
    talk_in = jnp.concatenate([got[8 * k : 8 * k + 8] for k in range(8)], axis=1) + talk_ref[...]
    inv = inverse(talk_in)
    own = (talk_in * gain_ref[...]).astype(BF16)
    gates = gates_of(dot(own, router_ref[...]) * inv, picks_ref[1], me)
    both = dot(own, up_ref[0]) * inv
    inner = (silu(both[:, :FT]) * both[:, FT:]).astype(BF16)
    reply = gates * dot(inner, down_ref[0]).astype(BF16).astype(F32)
    reply = reply + first_ref[:, :1] * talk_in
    reply = jnp.concatenate([reply, jnp.zeros_like(reply)], axis=0).astype(BF16)
    sent = dot(place_ref[...], reply)
    sent = [sent[:, 128 * k : 128 * k + 128].reshape(8, 8, 128) for k in range(8)]
    came = recv_ref[:, 64:, :].astype(F32).reshape(128, 128).astype(BF16)
    thinker = dot(carry_ref[...], came).reshape(8, 8, 128)
    out_ref[...] = jnp.concatenate(sent + [thinker], axis=1).astype(BF16)


def pass_kernel(recv_ref, out_ref, got_buf, buf):
    got_buf[...] = jnp.sum(recv_ref[...].astype(F32), axis=0)
    for side in range(2):
        for k in range(9):
            buf[side, 4 * k : 4 * k + 4, :] = got_buf[8 * k + 4 * side : 8 * k + 4 * side + 4, :]
        buf[side, 36:, :] = jnp.zeros((4, 128), F32)
    for d in range(16):
        out_ref[d] = buf[d >> 3].astype(BF16)


def finish_kernel(recv_ref, state_ref, thinker_ref, out_ref, buf):
    buf[...] = jnp.sum(recv_ref[:, :32, :].astype(F32), axis=0)
    for k in range(8):
        out_ref[:, 128 * k : 128 * k + 128] = buf[4 * k : 4 * k + 4, :]
    for d in range(16):
        cols = slice(128 * d, 128 * d + 128)
        thinker_ref[:, cols] = state_ref[:, cols] + recv_ref[d, 32:, :].astype(F32)[:OWN]


def call(kernel, outs, args, where, scratch=(), mib=16, flops=COST, outs_at=None):
    spaces = {"v": pltpu.VMEM, "s": pltpu.SMEM, "h": pltpu.HBM}
    many = isinstance(outs, list)
    whole = pl.BlockSpec(memory_space=pltpu.VMEM)
    return pl.pallas_call(
        kernel,
        out_shape=outs,
        in_specs=[pl.BlockSpec(memory_space=spaces[w]) for w in where],
        out_specs=[pl.BlockSpec(memory_space=spaces[w]) for w in outs_at or "v" * len(outs)] if many else whole,
        scratch_shapes=list(scratch),
        cost_estimate=pl.CostEstimate(flops=flops, bytes_accessed=1 << 20, transcendentals=0),
        compiler_params=pltpu.CompilerParams(vmem_limit_bytes=mib << 20),
    )(*args)


def array(shape, dtype):
    return jax.ShapeDtypeStruct(shape, dtype)


def exchange(msg, axis, groups=None):
    return lax.all_to_all(msg, axis, 0, 0, axis_index_groups=groups)


def on_device(
    queries,
    new_kv,
    kv_cache,
    lengths,
    out_proj,
    hidden_in,
    norm_gain,
    router,
    expert_ids,
    w_gate_up,
    w_down,
    talk_proj,
    talk_gain,
    talk_router,
    talk_ids,
    talk_gate_up,
    talk_down,
):
    both = ("seq", "exp")
    held = (lengths, queries, new_kv, expert_ids.T, talk_ids.T, kv_cache)
    msg, chosen, picks, sums, carry, place, first = call(
        attend_kernel,
        [
            array((SEQ, 16, 256), BF16),
            array((64, 256), BF16),
            array((2, 8, EXPERTS), F32),
            array((2, 128, 128), BF16),
            array((64, 128), BF16),
            array((64, 16), BF16),
            array((8, 128), F32),
        ],
        tuple(pltpu.with_memory_space_constraint(x, pltpu.HBM) for x in held),
        "hhhhhh",
        [
            pltpu.SMEM((OWN,), jnp.int32),
            pltpu.VMEM((OWN, HEADS * HD), BF16),
            pltpu.VMEM((2, OWN, KVH * HD), BF16),
            pltpu.VMEM((8, ROWS), jnp.int32),
            pltpu.VMEM((8, ROWS), jnp.int32),
            pltpu.VMEM((2, OWN, SPAN, KVH * HD), BF16),
            pltpu.VMEM((HEADS * OWN, HD), F32),
            pltpu.VMEM((HEADS * OWN, HD), F32),
            pltpu.VMEM((HEADS * OWN, HD), F32),
            pltpu.SemaphoreType.DMA((5 + 2 * OWN,)),
        ],
    )
    msg = call(
        project_kernel,
        array((SEQ, 16, 512), BF16),
        (exchange(msg, "seq"), out_proj),
        "vv",
        [pltpu.VMEM((16, 512), F32)],
    )
    msg, state = call(
        state_kernel,
        [array((EXP, 16, 512), BF16), array((OWN, D), F32)],
        (exchange(msg, "seq"), hidden_in),
        "vv",
        [pltpu.VMEM((16, 512), F32)],
    )
    msg, reply, talk_in = call(
        expert_kernel,
        [array((8, 16, 512), BF16), array((16, 8, 128), F32), array((8, DT), F32)],
        (
            exchange(msg, "exp").reshape(256, 512),
            chosen,
            picks,
            norm_gain.reshape(1, D),
            router,
            w_gate_up,
            w_down,
            talk_proj,
        ),
        "vvvvvvvv",
    )
    msg = call(
        route_kernel,
        array((16, 72, 128), BF16),
        (exchange(msg, both, NEAR).reshape(128, 512), sums, reply),
        "vvv",
    )
    msg = call(
        talker_kernel,
        array((8, 72, 128), BF16),
        (
            exchange(msg, both, FAR),
            talk_in,
            picks,
            carry,
            place,
            first,
            talk_gain.reshape(1, DT),
            talk_router,
            talk_gate_up,
            talk_down,
        ),
        "vvvvvvvvvv",
    )
    msg = call(
        pass_kernel,
        array((16, 40, 128), BF16),
        (exchange(msg, both, NEAR),),
        "v",
        [pltpu.VMEM((72, 128), F32), pltpu.VMEM((2, 40, 128), F32)],
    )
    thinker, talker = call(
        finish_kernel,
        [array((OWN, D), F32), array((OWN, DT), F32)],
        (exchange(msg, both, FAR), state),
        "vv",
        [pltpu.VMEM((32, 128), F32)],
    )
    return (thinker, talker)


def solution(mesh):
    placed = (
        P("exp", None),
        P(None, "exp", None),
        P(None, "exp", "seq", None),
        P("exp"),
        P("seq", None),
        P("exp", None),
        P(),
        P(),
        P(),
        P(("seq", "exp"), None, None),
        P(("seq", "exp"), None, None),
        P(),
        P(),
        P(),
        P(),
        P(("seq", "exp"), None, None),
        P(("seq", "exp"), None, None),
    )
    return jax.shard_map(
        on_device,
        mesh=mesh,
        in_specs=placed,
        out_specs=(P("exp", None), P("exp", None)),
        check_vma=False,
    )
```

```python
import functools
import jax
import jax.numpy as jnp
from jax import lax
from jax.experimental import pallas as pl
from jax.experimental.pallas import tpu as pltpu
from jax.sharding import PartitionSpec as P

F32 = jnp.float32
BF16 = jnp.bfloat16
HEADS = 32
KVH = 4
HD = 128
D = 2048
DT = 1024
FF = 768
FT = 384
EXPERTS = 128
ROWS = 64
SEQ = 8
EXP = 16
OWN = 4
SPAN = 512
EPS = 1e-6
COST = 10**11
NEG = -1e30


def iota(shape, dim):
    return lax.broadcasted_iota(jnp.int32, shape, dim)


def dot(a, b):
    return jnp.dot(a, b, preferred_element_type=F32)


def dot_t(a, b):
    return lax.dot_general(a, b, (((1,), (1,)), ((), ())), preferred_element_type=F32)


def my_expert():
    return lax.axis_index("seq") * EXP + lax.axis_index("exp")


def expert_of(far, near):
    return (far & 7) * EXP + (far >> 3) * 8 + near


def at(order, index):
    found = jnp.zeros_like(index)
    for k, member in enumerate(order):
        found = jnp.where(index == k, member, found)
    return found


SEQ_ORDER = (7, 6, 5, 4, 3, 1, 0, 2)
ALL_ORDER = (0, 1, 2, 3, 4, 5, 6, 7, 8, 9, 10, 11, 12, 13, 14, 15)
NEAR_ORDER = (1, 4, 2, 3, 7, 5, 6, 0)
FAR_ORDER = (2, 0, 14, 9, 3, 4, 8, 13, 11, 12, 7, 5, 15, 6, 1, 10)
NEAR = [[expert_of(far, near) for near in NEAR_ORDER] for far in range(16)]
FAR = [[expert_of(far, near) for far in FAR_ORDER] for near in range(8)]


def slots_by_row(ids, me):
    match = jnp.sum((ids == me).astype(F32), axis=0, keepdims=True)
    match = jnp.broadcast_to(match, (8, ROWS))
    before = (iota((ROWS, ROWS), 0) < iota((ROWS, ROWS), 1)).astype(F32)
    rank = dot(match, before)
    hit = jnp.logical_and(rank == iota((8, ROWS), 0).astype(F32), match > 0.5)
    return jnp.where(hit, 1.0, 0.0)


def slots_of(ids, experts, slot):
    match = jnp.zeros(experts.shape, F32)
    for k in range(ids.shape[0]):
        match = match + (ids[k : k + 1, :] == experts).astype(F32)
    before = (iota((ROWS, ROWS), 0) < iota((ROWS, ROWS), 1)).astype(F32)
    rank = dot(match, before)
    hit = jnp.logical_and(rank == slot.astype(F32), match > 0.5)
    return jnp.where(hit, 1.0, 0.0)


def spread_marks(count, bits):
    r = iota((ROWS, count), 0)
    i = iota((ROWS, count), 1)
    same = jnp.logical_and(at(ALL_ORDER, i >> (2 + bits)) == (r >> 2), (i & 3) == (r & 3))
    return jnp.where(same, 1.0, 0.0)


def by_chunk(marks, chunks):
    i = iota(marks.shape, 1)
    return jnp.concatenate(
        [jnp.where(((i >> 2) & (chunks - 1)) == j, marks, 0.0) for j in range(chunks)], axis=0
    )


def pick_marks(slots, ids):
    expert = iota((EXPERTS, ROWS), 0)
    named = jnp.zeros((EXPERTS, ROWS), F32)
    for k in range(ids.shape[0]):
        named = named + (ids[k : k + 1, :] == expert).astype(F32)
    return dot_t(slots, named)


def gates_of(logits, picks, me):
    sig = 1.0 / (1.0 + jnp.exp(-logits))
    total = jnp.sum(sig * picks, axis=1, keepdims=True)
    own = jnp.sum(jnp.where(iota(sig.shape, 1) == me, sig, 0.0), axis=1, keepdims=True)
    return jnp.where(total > 0.0, own / total, 0.0)


def silu(a):
    return a / (1.0 + jnp.exp(-a))


def start_all(pairs, sems):
    copies = []
    for k, (src, dst) in enumerate(pairs):
        copy = pltpu.make_async_copy(src, dst, sems.at[k])
        copy.start()
        copies.append(copy)
    return copies


def attend_kernel(
    len_hbm,
    q_hbm,
    new_hbm,
    ids_hbm,
    talk_hbm,
    kv_hbm,
    out_ref,
    chosen_ref,
    picks_ref,
    sums_ref,
    carry_ref,
    place_ref,
    first_ref,
    len_ref,
    q_ref,
    new_ref,
    ids_ref,
    talk_ref,
    kv_ref,
    q_buf,
    o_buf,
    t_buf,
    sems,
):
    pairs = [(q_hbm, q_ref), (ids_hbm, ids_ref), (talk_hbm, talk_ref), (new_hbm, new_ref), (len_hbm, len_ref)]
    pairs += [(kv_hbm.at[t, c], kv_ref.at[t, c]) for t in range(2) for c in range(OWN)]
    copies = start_all(pairs, sems)
    small, keys, values = copies[:5], copies[5 : 5 + OWN], copies[5 + OWN :]
    for copy in small:
        copy.wait()
    seq = lax.axis_index("seq")
    scale = HD ** (-0.5)
    query = q_ref[...].astype(F32)
    for h in range(HEADS):
        q_buf[4 * h : 4 * h + 4, :] = query[:, HD * h : HD * h + HD]

    me = my_expert()
    near = lax.axis_index("exp") & 7
    far = (lax.axis_index("exp") >> 3) * 8 + seq
    ids = ids_ref[...]
    talk_ids = talk_ref[...]
    slots = slots_by_row(ids, me)
    talk_slots = slots_by_row(talk_ids, me)
    picks_ref[0] = pick_marks(slots, ids)
    picks_ref[1] = pick_marks(talk_slots, talk_ids)
    both = jnp.concatenate([slots, talk_slots], axis=0)
    chosen_ref[...] = by_chunk(dot(both, spread_marks(256, 2)), 4).astype(BF16)
    first = (talk_ids[0:1, :] == me).astype(F32)
    first_ref[...] = dot_t(talk_slots, jnp.broadcast_to(first, (128, ROWS)))
    line = iota((128, ROWS), 0)
    came = slots_of(ids, expert_of(far, at(NEAR_ORDER, line >> 4)), line & 7)
    needed = slots_of(talk_ids, expert_of(at(FAR_ORDER, line >> 3), near), line & 7)
    half = (iota((128, 128), 1) >> 3) & 1
    sums = dot_t(needed, came)
    sums_ref[0] = jnp.where(half == 0, sums, 0.0).astype(BF16)
    sums_ref[1] = jnp.where(half == 1, sums, 0.0).astype(BF16)
    line = iota((ROWS, ROWS), 0)
    row = ((line >> 2) & 1) * 32 + at(NEAR_ORDER, line >> 3) * 4 + (line & 3)
    turn = jnp.where(row == iota((ROWS, ROWS), 1), 1.0, 0.0)
    line = iota((128, ROWS), 0)
    carry_ref[...] = dot_t(turn, slots_of(ids, expert_of(at(FAR_ORDER, line >> 3), near), line & 7)).astype(BF16)
    place_ref[...] = dot_t(turn, jnp.concatenate([talk_slots, jnp.zeros_like(talk_slots)], axis=0)).astype(BF16)

    lane = iota((HEADS, KVH * HD), 1)
    diag = (iota((HEADS, KVH * HD), 0) >> 3) == (lane >> 7)
    place = lane + seq * SPAN
    tail_lane = iota((HEADS, HD), 1)
    parts = []
    for c in range(OWN):
        q = q_buf[pl.ds(c, HEADS, stride=4), :]
        wide = jnp.where(diag, jnp.concatenate([q] * KVH, axis=1), 0.0)
        fresh_key = new_ref[0, c : c + 1, :].astype(F32)
        fresh = jnp.sum(wide * fresh_key, axis=1, keepdims=True) * scale
        parts.append((wide.astype(BF16), jnp.where(seq == 0, fresh, NEG)))
    for copy in keys:
        copy.wait()
    done = []
    for c in range(OWN):
        wide, fresh = parts[c]
        valid = place < len_ref[c]
        scores = jnp.where(valid, dot_t(wide, kv_ref[0, c]) * scale, NEG)
        peak = jnp.maximum(jnp.max(scores, axis=1, keepdims=True), fresh)
        peak = peak.astype(BF16).astype(F32)
        weights = jnp.where(valid, jnp.exp(scores - peak), 0.0).astype(BF16)
        fresh_weight = jnp.where(seq == 0, jnp.exp(fresh - peak), 0.0)
        total = jnp.sum(weights.astype(F32), axis=1, keepdims=True) + fresh_weight
        upper = total.astype(BF16).astype(F32)
        tail = jnp.where(tail_lane == 0, peak, jnp.where(tail_lane == 1, upper, total - upper))
        t_buf[pl.ds(c, HEADS, stride=4), :] = tail
        done.append((weights, fresh_weight))
    for copy in values:
        copy.wait()
    for c in range(OWN):
        weights, fresh_weight = done[c]
        fresh_value = new_ref[1, c : c + 1, :].astype(F32)
        mixed = dot(weights, kv_ref[1, c]) + fresh_weight * fresh_value
        mixed = jnp.where(diag, mixed, 0.0)
        mixed = (mixed[:, :HD] + mixed[:, HD : 2 * HD]) + (
            mixed[:, 2 * HD : 3 * HD] + mixed[:, 3 * HD :]
        )
        o_buf[pl.ds(c, HEADS, stride=4), :] = mixed
    for d, s in enumerate(SEQ_ORDER):
        out_ref[d, :, :HD] = o_buf[16 * s : 16 * s + 16, :].astype(BF16)
        out_ref[d, :, HD:] = t_buf[16 * s : 16 * s + 16, :].astype(BF16)


def project_kernel(recv_ref, proj_ref, out_ref, row_buf):
    got = recv_ref[...].astype(F32)
    peak = got[:, :, HD : HD + 1]
    total = got[:, :, HD + 1 : HD + 2] + got[:, :, HD + 2 : HD + 3]
    scale = jnp.exp(peak - jnp.max(peak, axis=0, keepdims=True))
    total = jnp.sum(scale * total, axis=0)
    mixed = jnp.sum(scale * got[:, :, :HD], axis=0) / total
    attn = jnp.concatenate([mixed[4 * h : 4 * h + 4] for h in range(4)], axis=1).astype(BF16)
    part = dot(attn, proj_ref[...])
    for j in range(4):
        row_buf[4 * j : 4 * j + 4, :] = part[:, 512 * j : 512 * j + 512]
    msg = row_buf[...].astype(BF16)
    for d in range(SEQ):
        out_ref[d] = msg


def state_kernel(recv_ref, hidden_ref, out_ref, rows_ref, buf):
    for j in range(4):
        buf[4 * j : 4 * j + 4, :] = hidden_ref[:, 512 * j : 512 * j + 512]
    buf[...] = buf[...] + jnp.sum(recv_ref[...].astype(F32), axis=0)
    msg = buf[...].astype(BF16)
    for d in range(EXP):
        out_ref[d] = msg
    for j in range(4):
        rows_ref[:, 512 * j : 512 * j + 512] = buf[4 * j : 4 * j + 4, :]


def inverse(stream):
    return lax.rsqrt(jnp.mean(stream * stream, axis=1, keepdims=True) + EPS)


def expert_kernel(
    recv_ref,
    chosen_ref,
    picks_ref,
    gain_ref,
    router_ref,
    up_ref,
    down_ref,
    proj_ref,
    out_ref,
    reply_ref,
    talk_ref,
):
    me = my_expert()
    rows = dot(chosen_ref[...], recv_ref[...])
    rows = jnp.concatenate([rows[16 * j : 16 * j + 16] for j in range(4)], axis=1)
    inv = inverse(rows[:8])
    own = (rows[:8] * gain_ref[...]).astype(BF16)
    gates = gates_of(dot(own, router_ref[...]) * inv, picks_ref[0], me)
    both = dot(own, up_ref[0]) * inv
    inner = (silu(both[:, :FF]) * both[:, FF:]).astype(BF16)
    reply = dot(inner, down_ref[0])
    reply = gates * reply.astype(BF16).astype(F32)
    mixed = dot(jnp.concatenate([reply, rows[8:]], axis=0).astype(BF16), proj_ref[...])
    talk_ref[...] = mixed[8:]
    msg = jnp.concatenate([mixed[:8, :512], mixed[:8, 512:]], axis=0).astype(BF16)
    for d in range(8):
        out_ref[d] = msg
    for d, far in enumerate(FAR_ORDER):
        reply_ref[d] = reply[:, 128 * far : 128 * far + 128]


def route_kernel(recv_ref, sums_ref, reply_ref, out_ref):
    upper = dot(sums_ref[0], recv_ref[...])
    lower = dot(sums_ref[1], recv_ref[...])
    talk = [upper[:, 128 * k : 128 * k + 128].reshape(16, 8, 128) for k in range(4)]
    talk += [lower[:, 128 * k : 128 * k + 128].reshape(16, 8, 128) for k in range(4)]
    out_ref[...] = jnp.concatenate(talk + [reply_ref[...]], axis=1).astype(BF16)


def talker_kernel(
    recv_ref,
    talk_ref,
    picks_ref,
    carry_ref,
    place_ref,
    first_ref,
    gain_ref,
    router_ref,
    up_ref,
    down_ref,
    out_ref,
):
    me = my_expert()
    got = jnp.sum(recv_ref[:, :64, :].astype(F32), axis=0)
    talk_in = jnp.concatenate([got[8 * k : 8 * k + 8] for k in range(8)], axis=1) + talk_ref[...]
    inv = inverse(talk_in)
    own = (talk_in * gain_ref[...]).astype(BF16)
    gates = gates_of(dot(own, router_ref[...]) * inv, picks_ref[1], me)
    both = dot(own, up_ref[0]) * inv
    inner = (silu(both[:, :FT]) * both[:, FT:]).astype(BF16)
    reply = gates * dot(inner, down_ref[0]).astype(BF16).astype(F32)
    reply = reply + first_ref[:, :1] * talk_in
    reply = jnp.concatenate([reply, jnp.zeros_like(reply)], axis=0).astype(BF16)
    sent = dot(place_ref[...], reply)
    sent = [sent[:, 128 * k : 128 * k + 128].reshape(8, 8, 128) for k in range(8)]
    came = recv_ref[:, 64:, :].astype(F32).reshape(128, 128).astype(BF16)
    thinker = dot(carry_ref[...], came).reshape(8, 8, 128)
    out_ref[...] = jnp.concatenate(sent + [thinker], axis=1).astype(BF16)


def pass_kernel(recv_ref, out_ref, got_buf, buf):
    got_buf[...] = jnp.sum(recv_ref[...].astype(F32), axis=0)
    for side in range(2):
        for k in range(9):
            buf[side, 4 * k : 4 * k + 4, :] = got_buf[8 * k + 4 * side : 8 * k + 4 * side + 4, :]
        buf[side, 36:, :] = jnp.zeros((4, 128), F32)
    for d, far in enumerate(FAR_ORDER):
        out_ref[d] = buf[far >> 3].astype(BF16)


def finish_kernel(recv_ref, state_ref, thinker_ref, out_ref, buf):
    buf[...] = jnp.sum(recv_ref[:, :32, :].astype(F32), axis=0)
    for k in range(8):
        out_ref[:, 128 * k : 128 * k + 128] = buf[4 * k : 4 * k + 4, :]
    for d, far in enumerate(FAR_ORDER):
        cols = slice(128 * far, 128 * far + 128)
        thinker_ref[:, cols] = state_ref[:, cols] + recv_ref[d, 32:, :].astype(F32)[:OWN]


def call(kernel, outs, args, where, scratch=(), mib=16, flops=COST, outs_at=None):
    spaces = {"v": pltpu.VMEM, "s": pltpu.SMEM, "h": pltpu.HBM}
    many = isinstance(outs, list)
    whole = pl.BlockSpec(memory_space=pltpu.VMEM)
    return pl.pallas_call(
        kernel,
        out_shape=outs,
        in_specs=[pl.BlockSpec(memory_space=spaces[w]) for w in where],
        out_specs=[pl.BlockSpec(memory_space=spaces[w]) for w in outs_at or "v" * len(outs)] if many else whole,
        scratch_shapes=list(scratch),
        cost_estimate=pl.CostEstimate(flops=flops, bytes_accessed=1 << 20, transcendentals=0),
        compiler_params=pltpu.CompilerParams(vmem_limit_bytes=mib << 20),
    )(*args)


def array(shape, dtype):
    return jax.ShapeDtypeStruct(shape, dtype)


def exchange(msg, axis, groups=None):
    return lax.all_to_all(msg, axis, 0, 0, axis_index_groups=groups)


def on_device(
    queries,
    new_kv,
    kv_cache,
    lengths,
    out_proj,
    hidden_in,
    norm_gain,
    router,
    expert_ids,
    w_gate_up,
    w_down,
    talk_proj,
    talk_gain,
    talk_router,
    talk_ids,
    talk_gate_up,
    talk_down,
):
    both = ("seq", "exp")
    held = (lengths, queries, new_kv, expert_ids.T, talk_ids.T, kv_cache)
    msg, chosen, picks, sums, carry, place, first = call(
        attend_kernel,
        [
            array((SEQ, 16, 256), BF16),
            array((64, 256), BF16),
            array((2, 8, EXPERTS), F32),
            array((2, 128, 128), BF16),
            array((64, 128), BF16),
            array((64, 16), BF16),
            array((8, 128), F32),
        ],
        tuple(pltpu.with_memory_space_constraint(x, pltpu.HBM) for x in held),
        "hhhhhh",
        [
            pltpu.SMEM((OWN,), jnp.int32),
            pltpu.VMEM((OWN, HEADS * HD), BF16),
            pltpu.VMEM((2, OWN, KVH * HD), BF16),
            pltpu.VMEM((8, ROWS), jnp.int32),
            pltpu.VMEM((8, ROWS), jnp.int32),
            pltpu.VMEM((2, OWN, SPAN, KVH * HD), BF16),
            pltpu.VMEM((HEADS * OWN, HD), F32),
            pltpu.VMEM((HEADS * OWN, HD), F32),
            pltpu.VMEM((HEADS * OWN, HD), F32),
            pltpu.SemaphoreType.DMA((5 + 2 * OWN,)),
        ],
    )
    msg = call(
        project_kernel,
        array((SEQ, 16, 512), BF16),
        (exchange(msg, "seq", [list(SEQ_ORDER)]), out_proj),
        "vv",
        [pltpu.VMEM((16, 512), F32)],
    )
    msg, state = call(
        state_kernel,
        [array((EXP, 16, 512), BF16), array((OWN, D), F32)],
        (exchange(msg, "seq", [list(SEQ_ORDER)]), hidden_in),
        "vv",
        [pltpu.VMEM((16, 512), F32)],
    )
    msg, reply, talk_in = call(
        expert_kernel,
        [array((8, 16, 512), BF16), array((16, 8, 128), F32), array((8, DT), F32)],
        (
            exchange(msg, "exp", [list(ALL_ORDER)]).reshape(256, 512),
            chosen,
            picks,
            norm_gain.reshape(1, D),
            router,
            w_gate_up,
            w_down,
            talk_proj,
        ),
        "vvvvvvvv",
    )
    msg = call(
        route_kernel,
        array((16, 72, 128), BF16),
        (exchange(msg, both, NEAR).reshape(128, 512), sums, reply),
        "vvv",
    )
    msg = call(
        talker_kernel,
        array((8, 72, 128), BF16),
        (
            exchange(msg, both, FAR),
            talk_in,
            picks,
            carry,
            place,
            first,
            talk_gain.reshape(1, DT),
            talk_router,
            talk_gate_up,
            talk_down,
        ),
        "vvvvvvvvvv",
    )
    msg = call(
        pass_kernel,
        array((16, 40, 128), BF16),
        (exchange(msg, both, NEAR),),
        "v",
        [pltpu.VMEM((72, 128), F32), pltpu.VMEM((2, 40, 128), F32)],
    )
    thinker, talker = call(
        finish_kernel,
        [array((OWN, D), F32), array((OWN, DT), F32)],
        (exchange(msg, both, FAR), state),
        "vv",
        [pltpu.VMEM((32, 128), F32)],
    )
    return (thinker, talker)


def solution(mesh):
    placed = (
        P("exp", None),
        P(None, "exp", None),
        P(None, "exp", "seq", None),
        P("exp"),
        P("seq", None),
        P("exp", None),
        P(),
        P(),
        P(),
        P(("seq", "exp"), None, None),
        P(("seq", "exp"), None, None),
        P(),
        P(),
        P(),
        P(),
        P(("seq", "exp"), None, None),
        P(("seq", "exp"), None, None),
    )
    return jax.shard_map(
        on_device,
        mesh=mesh,
        in_specs=placed,
        out_specs=(P("exp", None), P("exp", None)),
        check_vma=False,
    )
```

```python
import functools
import jax
import jax.numpy as jnp
from jax import lax
from jax.experimental import pallas as pl
from jax.experimental.pallas import tpu as pltpu
from jax.sharding import PartitionSpec as P

F32 = jnp.float32
BF16 = jnp.bfloat16
HEADS = 32
KVH = 4
HD = 128
D = 2048
DT = 1024
FF = 768
FT = 384
EXPERTS = 128
ROWS = 64
SEQ = 8
EXP = 16
OWN = 4
SPAN = 512
EPS = 1e-6
COST = 10**11
NEG = -1e30


def iota(shape, dim):
    return lax.broadcasted_iota(jnp.int32, shape, dim)


def dot(a, b):
    return jnp.dot(a, b, preferred_element_type=F32)


def dot_t(a, b):
    return lax.dot_general(a, b, (((1,), (1,)), ((), ())), preferred_element_type=F32)


def my_expert():
    return lax.axis_index("seq") * EXP + lax.axis_index("exp")


def expert_of(far, near):
    return (far & 7) * EXP + (far >> 3) * 8 + near


def at(order, index):
    found = jnp.zeros_like(index)
    for k, member in enumerate(order):
        found = jnp.where(index == k, member, found)
    return found


SEQ_ORDER = (7, 6, 5, 4, 3, 1, 0, 2)
ALL_ORDER = (0, 1, 2, 3, 4, 5, 6, 7, 8, 9, 10, 11, 12, 13, 14, 15)
NEAR_ORDER = (1, 0, 2, 3, 7, 5, 6, 4)
FAR_ORDER = (6, 1, 4, 0, 13, 10, 7, 14, 9, 2, 5, 12, 8, 15, 11, 3)
NEAR = [[expert_of(far, near) for near in NEAR_ORDER] for far in range(16)]
FAR = [[expert_of(far, near) for far in FAR_ORDER] for near in range(8)]


def slots_by_row(ids, me):
    match = jnp.sum((ids == me).astype(F32), axis=0, keepdims=True)
    match = jnp.broadcast_to(match, (8, ROWS))
    before = (iota((ROWS, ROWS), 0) < iota((ROWS, ROWS), 1)).astype(F32)
    rank = dot(match, before)
    hit = jnp.logical_and(rank == iota((8, ROWS), 0).astype(F32), match > 0.5)
    return jnp.where(hit, 1.0, 0.0)


def slots_of(ids, experts, slot):
    match = jnp.zeros(experts.shape, F32)
    for k in range(ids.shape[0]):
        match = match + (ids[k : k + 1, :] == experts).astype(F32)
    before = (iota((ROWS, ROWS), 0) < iota((ROWS, ROWS), 1)).astype(F32)
    rank = dot(match, before)
    hit = jnp.logical_and(rank == slot.astype(F32), match > 0.5)
    return jnp.where(hit, 1.0, 0.0)


def spread_marks(count, bits):
    r = iota((ROWS, count), 0)
    i = iota((ROWS, count), 1)
    same = jnp.logical_and(at(ALL_ORDER, i >> (2 + bits)) == (r >> 2), (i & 3) == (r & 3))
    return jnp.where(same, 1.0, 0.0)


def by_chunk(marks, chunks):
    i = iota(marks.shape, 1)
    return jnp.concatenate(
        [jnp.where(((i >> 2) & (chunks - 1)) == j, marks, 0.0) for j in range(chunks)], axis=0
    )


def pick_marks(slots, ids):
    expert = iota((EXPERTS, ROWS), 0)
    named = jnp.zeros((EXPERTS, ROWS), F32)
    for k in range(ids.shape[0]):
        named = named + (ids[k : k + 1, :] == expert).astype(F32)
    return dot_t(slots, named)


def gates_of(logits, picks, me):
    sig = 1.0 / (1.0 + jnp.exp(-logits))
    total = jnp.sum(sig * picks, axis=1, keepdims=True)
    own = jnp.sum(jnp.where(iota(sig.shape, 1) == me, sig, 0.0), axis=1, keepdims=True)
    return jnp.where(total > 0.0, own / total, 0.0)


def silu(a):
    return a / (1.0 + jnp.exp(-a))


def start_all(pairs, sems):
    copies = []
    for k, (src, dst) in enumerate(pairs):
        copy = pltpu.make_async_copy(src, dst, sems.at[k])
        copy.start()
        copies.append(copy)
    return copies


def attend_kernel(
    len_hbm,
    q_hbm,
    new_hbm,
    ids_hbm,
    talk_hbm,
    kv_hbm,
    out_ref,
    chosen_ref,
    picks_ref,
    sums_ref,
    carry_ref,
    place_ref,
    first_ref,
    len_ref,
    q_ref,
    new_ref,
    ids_ref,
    talk_ref,
    kv_ref,
    q_buf,
    o_buf,
    t_buf,
    sems,
):
    pairs = [(q_hbm, q_ref), (ids_hbm, ids_ref), (talk_hbm, talk_ref), (new_hbm, new_ref), (len_hbm, len_ref)]
    pairs += [(kv_hbm.at[t, c], kv_ref.at[t, c]) for t in range(2) for c in range(OWN)]
    copies = start_all(pairs, sems)
    small, keys, values = copies[:5], copies[5 : 5 + OWN], copies[5 + OWN :]
    for copy in small:
        copy.wait()
    seq = lax.axis_index("seq")
    scale = HD ** (-0.5)
    query = q_ref[...].astype(F32)
    for h in range(HEADS):
        q_buf[4 * h : 4 * h + 4, :] = query[:, HD * h : HD * h + HD]

    me = my_expert()
    near = lax.axis_index("exp") & 7
    far = (lax.axis_index("exp") >> 3) * 8 + seq
    ids = ids_ref[...]
    talk_ids = talk_ref[...]
    slots = slots_by_row(ids, me)
    talk_slots = slots_by_row(talk_ids, me)
    picks_ref[0] = pick_marks(slots, ids)
    picks_ref[1] = pick_marks(talk_slots, talk_ids)
    both = jnp.concatenate([slots, talk_slots], axis=0)
    chosen_ref[...] = by_chunk(dot(both, spread_marks(256, 2)), 4).astype(BF16)
    first = (talk_ids[0:1, :] == me).astype(F32)
    first_ref[...] = dot_t(talk_slots, jnp.broadcast_to(first, (128, ROWS)))
    line = iota((128, ROWS), 0)
    came = slots_of(ids, expert_of(far, at(NEAR_ORDER, line >> 4)), line & 7)
    needed = slots_of(talk_ids, expert_of(at(FAR_ORDER, line >> 3), near), line & 7)
    half = (iota((128, 128), 1) >> 3) & 1
    sums = dot_t(needed, came)
    sums_ref[0] = jnp.where(half == 0, sums, 0.0).astype(BF16)
    sums_ref[1] = jnp.where(half == 1, sums, 0.0).astype(BF16)
    line = iota((ROWS, ROWS), 0)
    row = ((line >> 2) & 1) * 32 + at(NEAR_ORDER, line >> 3) * 4 + (line & 3)
    turn = jnp.where(row == iota((ROWS, ROWS), 1), 1.0, 0.0)
    line = iota((128, ROWS), 0)
    carry_ref[...] = dot_t(turn, slots_of(ids, expert_of(at(FAR_ORDER, line >> 3), near), line & 7)).astype(BF16)
    place_ref[...] = dot_t(turn, jnp.concatenate([talk_slots, jnp.zeros_like(talk_slots)], axis=0)).astype(BF16)

    lane = iota((HEADS, KVH * HD), 1)
    diag = (iota((HEADS, KVH * HD), 0) >> 3) == (lane >> 7)
    place = lane + seq * SPAN
    tail_lane = iota((HEADS, HD), 1)
    parts = []
    for c in range(OWN):
        q = q_buf[pl.ds(c, HEADS, stride=4), :]
        wide = jnp.where(diag, jnp.concatenate([q] * KVH, axis=1), 0.0)
        fresh_key = new_ref[0, c : c + 1, :].astype(F32)
        fresh = jnp.sum(wide * fresh_key, axis=1, keepdims=True) * scale
        parts.append((wide.astype(BF16), jnp.where(seq == 0, fresh, NEG)))
    for copy in keys:
        copy.wait()
    done = []
    for c in range(OWN):
        wide, fresh = parts[c]
        valid = place < len_ref[c]
        scores = jnp.where(valid, dot_t(wide, kv_ref[0, c]) * scale, NEG)
        peak = jnp.maximum(jnp.max(scores, axis=1, keepdims=True), fresh)
        peak = peak.astype(BF16).astype(F32)
        weights = jnp.where(valid, jnp.exp(scores - peak), 0.0).astype(BF16)
        fresh_weight = jnp.where(seq == 0, jnp.exp(fresh - peak), 0.0)
        total = jnp.sum(weights.astype(F32), axis=1, keepdims=True) + fresh_weight
        upper = total.astype(BF16).astype(F32)
        tail = jnp.where(tail_lane == 0, peak, jnp.where(tail_lane == 1, upper, total - upper))
        t_buf[pl.ds(c, HEADS, stride=4), :] = tail
        done.append((weights, fresh_weight))
    for copy in values:
        copy.wait()
    for c in range(OWN):
        weights, fresh_weight = done[c]
        fresh_value = new_ref[1, c : c + 1, :].astype(F32)
        mixed = dot(weights, kv_ref[1, c]) + fresh_weight * fresh_value
        mixed = jnp.where(diag, mixed, 0.0)
        mixed = (mixed[:, :HD] + mixed[:, HD : 2 * HD]) + (
            mixed[:, 2 * HD : 3 * HD] + mixed[:, 3 * HD :]
        )
        o_buf[pl.ds(c, HEADS, stride=4), :] = mixed
    for d, s in enumerate(SEQ_ORDER):
        out_ref[d, :, :HD] = o_buf[16 * s : 16 * s + 16, :].astype(BF16)
        out_ref[d, :, HD:] = t_buf[16 * s : 16 * s + 16, :].astype(BF16)


def project_kernel(recv_ref, proj_ref, out_ref, row_buf):
    got = recv_ref[...].astype(F32)
    peak = got[:, :, HD : HD + 1]
    total = got[:, :, HD + 1 : HD + 2] + got[:, :, HD + 2 : HD + 3]
    scale = jnp.exp(peak - jnp.max(peak, axis=0, keepdims=True))
    total = jnp.sum(scale * total, axis=0)
    mixed = jnp.sum(scale * got[:, :, :HD], axis=0) / total
    attn = jnp.concatenate([mixed[4 * h : 4 * h + 4] for h in range(4)], axis=1).astype(BF16)
    part = dot(attn, proj_ref[...])
    for j in range(4):
        row_buf[4 * j : 4 * j + 4, :] = part[:, 512 * j : 512 * j + 512]
    msg = row_buf[...].astype(BF16)
    for d in range(SEQ):
        out_ref[d] = msg


def state_kernel(recv_ref, hidden_ref, out_ref, rows_ref, buf):
    for j in range(4):
        buf[4 * j : 4 * j + 4, :] = hidden_ref[:, 512 * j : 512 * j + 512]
    buf[...] = buf[...] + jnp.sum(recv_ref[...].astype(F32), axis=0)
    msg = buf[...].astype(BF16)
    for d in range(EXP):
        out_ref[d] = msg
    for j in range(4):
        rows_ref[:, 512 * j : 512 * j + 512] = buf[4 * j : 4 * j + 4, :]


def inverse(stream):
    return lax.rsqrt(jnp.mean(stream * stream, axis=1, keepdims=True) + EPS)


def expert_kernel(
    recv_ref,
    chosen_ref,
    picks_ref,
    gain_ref,
    router_ref,
    up_ref,
    down_ref,
    proj_ref,
    out_ref,
    reply_ref,
    talk_ref,
):
    me = my_expert()
    rows = dot(chosen_ref[...], recv_ref[...])
    rows = jnp.concatenate([rows[16 * j : 16 * j + 16] for j in range(4)], axis=1)
    inv = inverse(rows[:8])
    own = (rows[:8] * gain_ref[...]).astype(BF16)
    gates = gates_of(dot(own, router_ref[...]) * inv, picks_ref[0], me)
    both = dot(own, up_ref[0]) * inv
    inner = (silu(both[:, :FF]) * both[:, FF:]).astype(BF16)
    reply = dot(inner, down_ref[0])
    reply = gates * reply.astype(BF16).astype(F32)
    mixed = dot(jnp.concatenate([reply, rows[8:]], axis=0).astype(BF16), proj_ref[...])
    talk_ref[...] = mixed[8:]
    msg = jnp.concatenate([mixed[:8, :512], mixed[:8, 512:]], axis=0).astype(BF16)
    for d in range(8):
        out_ref[d] = msg
    for d, far in enumerate(FAR_ORDER):
        reply_ref[d] = reply[:, 128 * far : 128 * far + 128]


def route_kernel(recv_ref, sums_ref, reply_ref, out_ref):
    upper = dot(sums_ref[0], recv_ref[...])
    lower = dot(sums_ref[1], recv_ref[...])
    talk = [upper[:, 128 * k : 128 * k + 128].reshape(16, 8, 128) for k in range(4)]
    talk += [lower[:, 128 * k : 128 * k + 128].reshape(16, 8, 128) for k in range(4)]
    out_ref[...] = jnp.concatenate(talk + [reply_ref[...]], axis=1).astype(BF16)


def talker_kernel(
    recv_ref,
    talk_ref,
    picks_ref,
    carry_ref,
    place_ref,
    first_ref,
    gain_ref,
    router_ref,
    up_ref,
    down_ref,
    out_ref,
):
    me = my_expert()
    got = jnp.sum(recv_ref[:, :64, :].astype(F32), axis=0)
    talk_in = jnp.concatenate([got[8 * k : 8 * k + 8] for k in range(8)], axis=1) + talk_ref[...]
    inv = inverse(talk_in)
    own = (talk_in * gain_ref[...]).astype(BF16)
    gates = gates_of(dot(own, router_ref[...]) * inv, picks_ref[1], me)
    both = dot(own, up_ref[0]) * inv
    inner = (silu(both[:, :FT]) * both[:, FT:]).astype(BF16)
    reply = gates * dot(inner, down_ref[0]).astype(BF16).astype(F32)
    reply = reply + first_ref[:, :1] * talk_in
    reply = jnp.concatenate([reply, jnp.zeros_like(reply)], axis=0).astype(BF16)
    sent = dot(place_ref[...], reply)
    sent = [sent[:, 128 * k : 128 * k + 128].reshape(8, 8, 128) for k in range(8)]
    came = recv_ref[:, 64:, :].astype(F32).reshape(128, 128).astype(BF16)
    thinker = dot(carry_ref[...], came).reshape(8, 8, 128)
    out_ref[...] = jnp.concatenate(sent + [thinker], axis=1).astype(BF16)


def pass_kernel(recv_ref, out_ref, got_buf, buf):
    got_buf[...] = jnp.sum(recv_ref[...].astype(F32), axis=0)
    for side in range(2):
        for k in range(9):
            buf[side, 4 * k : 4 * k + 4, :] = got_buf[8 * k + 4 * side : 8 * k + 4 * side + 4, :]
        buf[side, 36:, :] = jnp.zeros((4, 128), F32)
    for d, far in enumerate(FAR_ORDER):
        out_ref[d] = buf[far >> 3].astype(BF16)


def finish_kernel(recv_ref, state_ref, thinker_ref, out_ref, buf):
    buf[...] = jnp.sum(recv_ref[:, :32, :].astype(F32), axis=0)
    for k in range(8):
        out_ref[:, 128 * k : 128 * k + 128] = buf[4 * k : 4 * k + 4, :]
    for d, far in enumerate(FAR_ORDER):
        cols = slice(128 * far, 128 * far + 128)
        thinker_ref[:, cols] = state_ref[:, cols] + recv_ref[d, 32:, :].astype(F32)[:OWN]


def call(kernel, outs, args, where, scratch=(), mib=16, flops=COST, outs_at=None):
    spaces = {"v": pltpu.VMEM, "s": pltpu.SMEM, "h": pltpu.HBM}
    many = isinstance(outs, list)
    whole = pl.BlockSpec(memory_space=pltpu.VMEM)
    return pl.pallas_call(
        kernel,
        out_shape=outs,
        in_specs=[pl.BlockSpec(memory_space=spaces[w]) for w in where],
        out_specs=[pl.BlockSpec(memory_space=spaces[w]) for w in outs_at or "v" * len(outs)] if many else whole,
        scratch_shapes=list(scratch),
        cost_estimate=pl.CostEstimate(flops=flops, bytes_accessed=1 << 20, transcendentals=0),
        compiler_params=pltpu.CompilerParams(vmem_limit_bytes=mib << 20),
    )(*args)


def array(shape, dtype):
    return jax.ShapeDtypeStruct(shape, dtype)


def exchange(msg, axis, groups=None):
    return lax.all_to_all(msg, axis, 0, 0, axis_index_groups=groups)


def on_device(
    queries,
    new_kv,
    kv_cache,
    lengths,
    out_proj,
    hidden_in,
    norm_gain,
    router,
    expert_ids,
    w_gate_up,
    w_down,
    talk_proj,
    talk_gain,
    talk_router,
    talk_ids,
    talk_gate_up,
    talk_down,
):
    both = ("seq", "exp")
    held = (lengths, queries, new_kv, expert_ids.T, talk_ids.T, kv_cache)
    msg, chosen, picks, sums, carry, place, first = call(
        attend_kernel,
        [
            array((SEQ, 16, 256), BF16),
            array((64, 256), BF16),
            array((2, 8, EXPERTS), F32),
            array((2, 128, 128), BF16),
            array((64, 128), BF16),
            array((64, 16), BF16),
            array((8, 128), F32),
        ],
        tuple(pltpu.with_memory_space_constraint(x, pltpu.HBM) for x in held),
        "hhhhhh",
        [
            pltpu.SMEM((OWN,), jnp.int32),
            pltpu.VMEM((OWN, HEADS * HD), BF16),
            pltpu.VMEM((2, OWN, KVH * HD), BF16),
            pltpu.VMEM((8, ROWS), jnp.int32),
            pltpu.VMEM((8, ROWS), jnp.int32),
            pltpu.VMEM((2, OWN, SPAN, KVH * HD), BF16),
            pltpu.VMEM((HEADS * OWN, HD), F32),
            pltpu.VMEM((HEADS * OWN, HD), F32),
            pltpu.VMEM((HEADS * OWN, HD), F32),
            pltpu.SemaphoreType.DMA((5 + 2 * OWN,)),
        ],
    )
    msg = call(
        project_kernel,
        array((SEQ, 16, 512), BF16),
        (exchange(msg, "seq", [list(SEQ_ORDER)]), out_proj),
        "vv",
        [pltpu.VMEM((16, 512), F32)],
    )
    msg, state = call(
        state_kernel,
        [array((EXP, 16, 512), BF16), array((OWN, D), F32)],
        (exchange(msg, "seq", [list(SEQ_ORDER)]), hidden_in),
        "vv",
        [pltpu.VMEM((16, 512), F32)],
    )
    msg, reply, talk_in = call(
        expert_kernel,
        [array((8, 16, 512), BF16), array((16, 8, 128), F32), array((8, DT), F32)],
        (
            exchange(msg, "exp", [list(ALL_ORDER)]).reshape(256, 512),
            chosen,
            picks,
            norm_gain.reshape(1, D),
            router,
            w_gate_up,
            w_down,
            talk_proj,
        ),
        "vvvvvvvv",
    )
    msg = call(
        route_kernel,
        array((16, 72, 128), BF16),
        (exchange(msg, both, NEAR).reshape(128, 512), sums, reply),
        "vvv",
    )
    msg = call(
        talker_kernel,
        array((8, 72, 128), BF16),
        (
            exchange(msg, both, FAR),
            talk_in,
            picks,
            carry,
            place,
            first,
            talk_gain.reshape(1, DT),
            talk_router,
            talk_gate_up,
            talk_down,
        ),
        "vvvvvvvvvv",
    )
    msg = call(
        pass_kernel,
        array((16, 40, 128), BF16),
        (exchange(msg, both, NEAR),),
        "v",
        [pltpu.VMEM((72, 128), F32), pltpu.VMEM((2, 40, 128), F32)],
    )
    thinker, talker = call(
        finish_kernel,
        [array((OWN, D), F32), array((OWN, DT), F32)],
        (exchange(msg, both, FAR), state),
        "vv",
        [pltpu.VMEM((32, 128), F32)],
    )
    return (thinker, talker)


def solution(mesh):
    placed = (
        P("exp", None),
        P(None, "exp", None),
        P(None, "exp", "seq", None),
        P("exp"),
        P("seq", None),
        P("exp", None),
        P(),
        P(),
        P(),
        P(("seq", "exp"), None, None),
        P(("seq", "exp"), None, None),
        P(),
        P(),
        P(),
        P(),
        P(("seq", "exp"), None, None),
        P(("seq", "exp"), None, None),
    )
    return jax.shard_map(
        on_device,
        mesh=mesh,
        in_specs=placed,
        out_specs=(P("exp", None), P("exp", None)),
        check_vma=False,
    )
```

```python
import functools
import jax
import jax.numpy as jnp
from jax import lax
from jax.experimental import pallas as pl
from jax.experimental.pallas import tpu as pltpu
from jax.sharding import PartitionSpec as P

F32 = jnp.float32
BF16 = jnp.bfloat16
HEADS = 32
KVH = 4
HD = 128
D = 2048
DT = 1024
FF = 768
FT = 384
EXPERTS = 128
ROWS = 64
SEQ = 8
EXP = 16
OWN = 4
SPAN = 512
EPS = 1e-6
COST = 10**11
NEG = -1e30


def iota(shape, dim):
    return lax.broadcasted_iota(jnp.int32, shape, dim)


def dot(a, b):
    return jnp.dot(a, b, preferred_element_type=F32)


def dot_t(a, b):
    return lax.dot_general(a, b, (((1,), (1,)), ((), ())), preferred_element_type=F32)


def my_expert():
    return lax.axis_index("seq") * EXP + lax.axis_index("exp")


def expert_of(far, near):
    return (far & 7) * EXP + (far >> 3) * 8 + near


def at(order, index):
    found = jnp.zeros_like(index)
    for k, member in enumerate(order):
        found = jnp.where(index == k, member, found)
    return found


SEQ_ORDER = (7, 6, 5, 4, 3, 1, 0, 2)
ALL_ORDER = (4, 1, 2, 3, 0, 5, 6, 7, 8, 9, 10, 11, 12, 13, 14, 15)
NEAR_ORDER = (5, 7, 0, 3, 6, 1, 4, 2)
FAR_ORDER = (6, 1, 4, 0, 13, 10, 7, 14, 9, 2, 5, 12, 8, 15, 11, 3)
NEAR = [[expert_of(far, near) for near in NEAR_ORDER] for far in range(16)]
FAR = [[expert_of(far, near) for far in FAR_ORDER] for near in range(8)]


def slots_by_row(ids, me):
    match = jnp.sum((ids == me).astype(F32), axis=0, keepdims=True)
    match = jnp.broadcast_to(match, (8, ROWS))
    before = (iota((ROWS, ROWS), 0) < iota((ROWS, ROWS), 1)).astype(F32)
    rank = dot(match, before)
    hit = jnp.logical_and(rank == iota((8, ROWS), 0).astype(F32), match > 0.5)
    return jnp.where(hit, 1.0, 0.0)


def slots_of(ids, experts, slot):
    match = jnp.zeros(experts.shape, F32)
    for k in range(ids.shape[0]):
        match = match + (ids[k : k + 1, :] == experts).astype(F32)
    before = (iota((ROWS, ROWS), 0) < iota((ROWS, ROWS), 1)).astype(F32)
    rank = dot(match, before)
    hit = jnp.logical_and(rank == slot.astype(F32), match > 0.5)
    return jnp.where(hit, 1.0, 0.0)


def spread_marks(count, bits):
    r = iota((ROWS, count), 0)
    i = iota((ROWS, count), 1)
    same = jnp.logical_and(at(ALL_ORDER, i >> (2 + bits)) == (r >> 2), (i & 3) == (r & 3))
    return jnp.where(same, 1.0, 0.0)


def by_chunk(marks, chunks):
    i = iota(marks.shape, 1)
    return jnp.concatenate(
        [jnp.where(((i >> 2) & (chunks - 1)) == j, marks, 0.0) for j in range(chunks)], axis=0
    )


def pick_marks(slots, ids):
    expert = iota((EXPERTS, ROWS), 0)
    named = jnp.zeros((EXPERTS, ROWS), F32)
    for k in range(ids.shape[0]):
        named = named + (ids[k : k + 1, :] == expert).astype(F32)
    return dot_t(slots, named)


def gates_of(logits, picks, me):
    sig = 1.0 / (1.0 + jnp.exp(-logits))
    total = jnp.sum(sig * picks, axis=1, keepdims=True)
    own = jnp.sum(jnp.where(iota(sig.shape, 1) == me, sig, 0.0), axis=1, keepdims=True)
    return jnp.where(total > 0.0, own / total, 0.0)


def silu(a):
    return a / (1.0 + jnp.exp(-a))


def start_all(pairs, sems):
    copies = []
    for k, (src, dst) in enumerate(pairs):
        copy = pltpu.make_async_copy(src, dst, sems.at[k])
        copy.start()
        copies.append(copy)
    return copies


def attend_kernel(
    len_hbm,
    q_hbm,
    new_hbm,
    ids_hbm,
    talk_hbm,
    kv_hbm,
    out_ref,
    chosen_ref,
    picks_ref,
    sums_ref,
    carry_ref,
    place_ref,
    first_ref,
    len_ref,
    q_ref,
    new_ref,
    ids_ref,
    talk_ref,
    kv_ref,
    q_buf,
    o_buf,
    t_buf,
    sems,
):
    pairs = [(q_hbm, q_ref), (ids_hbm, ids_ref), (talk_hbm, talk_ref), (new_hbm, new_ref), (len_hbm, len_ref)]
    pairs += [(kv_hbm.at[t, c], kv_ref.at[t, c]) for t in range(2) for c in range(OWN)]
    copies = start_all(pairs, sems)
    small, keys, values = copies[:5], copies[5 : 5 + OWN], copies[5 + OWN :]
    for copy in small:
        copy.wait()
    seq = lax.axis_index("seq")
    scale = HD ** (-0.5)
    query = q_ref[...].astype(F32)
    for h in range(HEADS):
        q_buf[4 * h : 4 * h + 4, :] = query[:, HD * h : HD * h + HD]

    me = my_expert()
    near = lax.axis_index("exp") & 7
    far = (lax.axis_index("exp") >> 3) * 8 + seq
    ids = ids_ref[...]
    talk_ids = talk_ref[...]
    slots = slots_by_row(ids, me)
    talk_slots = slots_by_row(talk_ids, me)
    picks_ref[0] = pick_marks(slots, ids)
    picks_ref[1] = pick_marks(talk_slots, talk_ids)
    both = jnp.concatenate([slots, talk_slots], axis=0)
    chosen_ref[...] = by_chunk(dot(both, spread_marks(256, 2)), 4).astype(BF16)
    first = (talk_ids[0:1, :] == me).astype(F32)
    first_ref[...] = dot_t(talk_slots, jnp.broadcast_to(first, (128, ROWS)))
    line = iota((128, ROWS), 0)
    came = slots_of(ids, expert_of(far, at(NEAR_ORDER, line >> 4)), line & 7)
    needed = slots_of(talk_ids, expert_of(at(FAR_ORDER, line >> 3), near), line & 7)
    half = (iota((128, 128), 1) >> 3) & 1
    sums = dot_t(needed, came)
    sums_ref[0] = jnp.where(half == 0, sums, 0.0).astype(BF16)
    sums_ref[1] = jnp.where(half == 1, sums, 0.0).astype(BF16)
    line = iota((ROWS, ROWS), 0)
    row = ((line >> 2) & 1) * 32 + at(NEAR_ORDER, line >> 3) * 4 + (line & 3)
    turn = jnp.where(row == iota((ROWS, ROWS), 1), 1.0, 0.0)
    line = iota((128, ROWS), 0)
    carry_ref[...] = dot_t(turn, slots_of(ids, expert_of(at(FAR_ORDER, line >> 3), near), line & 7)).astype(BF16)
    place_ref[...] = dot_t(turn, jnp.concatenate([talk_slots, jnp.zeros_like(talk_slots)], axis=0)).astype(BF16)

    lane = iota((HEADS, KVH * HD), 1)
    diag = (iota((HEADS, KVH * HD), 0) >> 3) == (lane >> 7)
    place = lane + seq * SPAN
    tail_lane = iota((HEADS, HD), 1)
    parts = []
    for c in range(OWN):
        q = q_buf[pl.ds(c, HEADS, stride=4), :]
        wide = jnp.where(diag, jnp.concatenate([q] * KVH, axis=1), 0.0)
        fresh_key = new_ref[0, c : c + 1, :].astype(F32)
        fresh = jnp.sum(wide * fresh_key, axis=1, keepdims=True) * scale
        parts.append((wide.astype(BF16), jnp.where(seq == 0, fresh, NEG)))
    for copy in keys:
        copy.wait()
    done = []
    for c in range(OWN):
        wide, fresh = parts[c]
        valid = place < len_ref[c]
        scores = jnp.where(valid, dot_t(wide, kv_ref[0, c]) * scale, NEG)
        peak = jnp.maximum(jnp.max(scores, axis=1, keepdims=True), fresh)
        peak = peak.astype(BF16).astype(F32)
        weights = jnp.where(valid, jnp.exp(scores - peak), 0.0).astype(BF16)
        fresh_weight = jnp.where(seq == 0, jnp.exp(fresh - peak), 0.0)
        total = jnp.sum(weights.astype(F32), axis=1, keepdims=True) + fresh_weight
        upper = total.astype(BF16).astype(F32)
        tail = jnp.where(tail_lane == 0, peak, jnp.where(tail_lane == 1, upper, total - upper))
        t_buf[pl.ds(c, HEADS, stride=4), :] = tail
        done.append((weights, fresh_weight))
    for copy in values:
        copy.wait()
    for c in range(OWN):
        weights, fresh_weight = done[c]
        fresh_value = new_ref[1, c : c + 1, :].astype(F32)
        mixed = dot(weights, kv_ref[1, c]) + fresh_weight * fresh_value
        mixed = jnp.where(diag, mixed, 0.0)
        mixed = (mixed[:, :HD] + mixed[:, HD : 2 * HD]) + (
            mixed[:, 2 * HD : 3 * HD] + mixed[:, 3 * HD :]
        )
        o_buf[pl.ds(c, HEADS, stride=4), :] = mixed
    for d, s in enumerate(SEQ_ORDER):
        out_ref[d, :, :HD] = o_buf[16 * s : 16 * s + 16, :].astype(BF16)
        out_ref[d, :, HD:] = t_buf[16 * s : 16 * s + 16, :].astype(BF16)


def project_kernel(recv_ref, proj_ref, out_ref, row_buf):
    got = recv_ref[...].astype(F32)
    peak = got[:, :, HD : HD + 1]
    total = got[:, :, HD + 1 : HD + 2] + got[:, :, HD + 2 : HD + 3]
    scale = jnp.exp(peak - jnp.max(peak, axis=0, keepdims=True))
    total = jnp.sum(scale * total, axis=0)
    mixed = jnp.sum(scale * got[:, :, :HD], axis=0) / total
    attn = jnp.concatenate([mixed[4 * h : 4 * h + 4] for h in range(4)], axis=1).astype(BF16)
    part = dot(attn, proj_ref[...])
    for j in range(4):
        row_buf[4 * j : 4 * j + 4, :] = part[:, 512 * j : 512 * j + 512]
    msg = row_buf[...].astype(BF16)
    for d in range(SEQ):
        out_ref[d] = msg


def state_kernel(recv_ref, hidden_ref, out_ref, rows_ref, buf):
    for j in range(4):
        buf[4 * j : 4 * j + 4, :] = hidden_ref[:, 512 * j : 512 * j + 512]
    buf[...] = buf[...] + jnp.sum(recv_ref[...].astype(F32), axis=0)
    msg = buf[...].astype(BF16)
    for d in range(EXP):
        out_ref[d] = msg
    for j in range(4):
        rows_ref[:, 512 * j : 512 * j + 512] = buf[4 * j : 4 * j + 4, :]


def inverse(stream):
    return lax.rsqrt(jnp.mean(stream * stream, axis=1, keepdims=True) + EPS)


def expert_kernel(
    recv_ref,
    chosen_ref,
    picks_ref,
    gain_ref,
    router_ref,
    up_ref,
    down_ref,
    proj_ref,
    out_ref,
    reply_ref,
    talk_ref,
):
    me = my_expert()
    rows = dot(chosen_ref[...], recv_ref[...])
    rows = jnp.concatenate([rows[16 * j : 16 * j + 16] for j in range(4)], axis=1)
    inv = inverse(rows[:8])
    own = (rows[:8] * gain_ref[...]).astype(BF16)
    gates = gates_of(dot(own, router_ref[...]) * inv, picks_ref[0], me)
    both = dot(own, up_ref[0]) * inv
    inner = (silu(both[:, :FF]) * both[:, FF:]).astype(BF16)
    reply = dot(inner, down_ref[0])
    reply = gates * reply.astype(BF16).astype(F32)
    mixed = dot(jnp.concatenate([reply, rows[8:]], axis=0).astype(BF16), proj_ref[...])
    talk_ref[...] = mixed[8:]
    msg = jnp.concatenate([mixed[:8, :512], mixed[:8, 512:]], axis=0).astype(BF16)
    for d in range(8):
        out_ref[d] = msg
    for d, far in enumerate(FAR_ORDER):
        reply_ref[d] = reply[:, 128 * far : 128 * far + 128]


def route_kernel(recv_ref, sums_ref, reply_ref, out_ref):
    upper = dot(sums_ref[0], recv_ref[...])
    lower = dot(sums_ref[1], recv_ref[...])
    talk = [upper[:, 128 * k : 128 * k + 128].reshape(16, 8, 128) for k in range(4)]
    talk += [lower[:, 128 * k : 128 * k + 128].reshape(16, 8, 128) for k in range(4)]
    out_ref[...] = jnp.concatenate(talk + [reply_ref[...]], axis=1).astype(BF16)


def talker_kernel(
    recv_ref,
    talk_ref,
    picks_ref,
    carry_ref,
    place_ref,
    first_ref,
    gain_ref,
    router_ref,
    up_ref,
    down_ref,
    out_ref,
):
    me = my_expert()
    got = jnp.sum(recv_ref[:, :64, :].astype(F32), axis=0)
    talk_in = jnp.concatenate([got[8 * k : 8 * k + 8] for k in range(8)], axis=1) + talk_ref[...]
    inv = inverse(talk_in)
    own = (talk_in * gain_ref[...]).astype(BF16)
    gates = gates_of(dot(own, router_ref[...]) * inv, picks_ref[1], me)
    both = dot(own, up_ref[0]) * inv
    inner = (silu(both[:, :FT]) * both[:, FT:]).astype(BF16)
    reply = gates * dot(inner, down_ref[0]).astype(BF16).astype(F32)
    reply = reply + first_ref[:, :1] * talk_in
    reply = jnp.concatenate([reply, jnp.zeros_like(reply)], axis=0).astype(BF16)
    sent = dot(place_ref[...], reply)
    sent = [sent[:, 128 * k : 128 * k + 128].reshape(8, 8, 128) for k in range(8)]
    came = recv_ref[:, 64:, :].astype(F32).reshape(128, 128).astype(BF16)
    thinker = dot(carry_ref[...], came).reshape(8, 8, 128)
    out_ref[...] = jnp.concatenate(sent + [thinker], axis=1).astype(BF16)


def pass_kernel(recv_ref, out_ref, got_buf, buf):
    got_buf[...] = jnp.sum(recv_ref[...].astype(F32), axis=0)
    for side in range(2):
        for k in range(9):
            buf[side, 4 * k : 4 * k + 4, :] = got_buf[8 * k + 4 * side : 8 * k + 4 * side + 4, :]
        buf[side, 36:, :] = jnp.zeros((4, 128), F32)
    for d, far in enumerate(FAR_ORDER):
        out_ref[d] = buf[far >> 3].astype(BF16)


def finish_kernel(recv_ref, state_ref, thinker_ref, out_ref, buf):
    buf[...] = jnp.sum(recv_ref[:, :32, :].astype(F32), axis=0)
    for k in range(8):
        out_ref[:, 128 * k : 128 * k + 128] = buf[4 * k : 4 * k + 4, :]
    for d, far in enumerate(FAR_ORDER):
        cols = slice(128 * far, 128 * far + 128)
        thinker_ref[:, cols] = state_ref[:, cols] + recv_ref[d, 32:, :].astype(F32)[:OWN]


def call(kernel, outs, args, where, scratch=(), mib=16, flops=COST, outs_at=None):
    spaces = {"v": pltpu.VMEM, "s": pltpu.SMEM, "h": pltpu.HBM}
    many = isinstance(outs, list)
    whole = pl.BlockSpec(memory_space=pltpu.VMEM)
    return pl.pallas_call(
        kernel,
        out_shape=outs,
        in_specs=[pl.BlockSpec(memory_space=spaces[w]) for w in where],
        out_specs=[pl.BlockSpec(memory_space=spaces[w]) for w in outs_at or "v" * len(outs)] if many else whole,
        scratch_shapes=list(scratch),
        cost_estimate=pl.CostEstimate(flops=flops, bytes_accessed=1 << 20, transcendentals=0),
        compiler_params=pltpu.CompilerParams(vmem_limit_bytes=mib << 20),
    )(*args)


def array(shape, dtype):
    return jax.ShapeDtypeStruct(shape, dtype)


def exchange(msg, axis, groups=None):
    return lax.all_to_all(msg, axis, 0, 0, axis_index_groups=groups)


def on_device(
    queries,
    new_kv,
    kv_cache,
    lengths,
    out_proj,
    hidden_in,
    norm_gain,
    router,
    expert_ids,
    w_gate_up,
    w_down,
    talk_proj,
    talk_gain,
    talk_router,
    talk_ids,
    talk_gate_up,
    talk_down,
):
    both = ("seq", "exp")
    held = (lengths, queries, new_kv, expert_ids.T, talk_ids.T, kv_cache)
    msg, chosen, picks, sums, carry, place, first = call(
        attend_kernel,
        [
            array((SEQ, 16, 256), BF16),
            array((64, 256), BF16),
            array((2, 8, EXPERTS), F32),
            array((2, 128, 128), BF16),
            array((64, 128), BF16),
            array((64, 16), BF16),
            array((8, 128), F32),
        ],
        tuple(pltpu.with_memory_space_constraint(x, pltpu.HBM) for x in held),
        "hhhhhh",
        [
            pltpu.SMEM((OWN,), jnp.int32),
            pltpu.VMEM((OWN, HEADS * HD), BF16),
            pltpu.VMEM((2, OWN, KVH * HD), BF16),
            pltpu.VMEM((8, ROWS), jnp.int32),
            pltpu.VMEM((8, ROWS), jnp.int32),
            pltpu.VMEM((2, OWN, SPAN, KVH * HD), BF16),
            pltpu.VMEM((HEADS * OWN, HD), F32),
            pltpu.VMEM((HEADS * OWN, HD), F32),
            pltpu.VMEM((HEADS * OWN, HD), F32),
            pltpu.SemaphoreType.DMA((5 + 2 * OWN,)),
        ],
    )
    msg = call(
        project_kernel,
        array((SEQ, 16, 512), BF16),
        (exchange(msg, "seq", [list(SEQ_ORDER)]), out_proj),
        "vv",
        [pltpu.VMEM((16, 512), F32)],
    )
    msg, state = call(
        state_kernel,
        [array((EXP, 16, 512), BF16), array((OWN, D), F32)],
        (exchange(msg, "seq", [list(SEQ_ORDER)]), hidden_in),
        "vv",
        [pltpu.VMEM((16, 512), F32)],
    )
    msg, reply, talk_in = call(
        expert_kernel,
        [array((8, 16, 512), BF16), array((16, 8, 128), F32), array((8, DT), F32)],
        (
            exchange(msg, "exp", [list(ALL_ORDER)]).reshape(256, 512),
            chosen,
            picks,
            norm_gain.reshape(1, D),
            router,
            w_gate_up,
            w_down,
            talk_proj,
        ),
        "vvvvvvvv",
    )
    msg = call(
        route_kernel,
        array((16, 72, 128), BF16),
        (exchange(msg, both, NEAR).reshape(128, 512), sums, reply),
        "vvv",
    )
    msg = call(
        talker_kernel,
        array((8, 72, 128), BF16),
        (
            exchange(msg, both, FAR),
            talk_in,
            picks,
            carry,
            place,
            first,
            talk_gain.reshape(1, DT),
            talk_router,
            talk_gate_up,
            talk_down,
        ),
        "vvvvvvvvvv",
    )
    msg = call(
        pass_kernel,
        array((16, 40, 128), BF16),
        (exchange(msg, both, NEAR),),
        "v",
        [pltpu.VMEM((72, 128), F32), pltpu.VMEM((2, 40, 128), F32)],
    )
    thinker, talker = call(
        finish_kernel,
        [array((OWN, D), F32), array((OWN, DT), F32)],
        (exchange(msg, both, FAR), state),
        "vv",
        [pltpu.VMEM((32, 128), F32)],
    )
    return (thinker, talker)


def solution(mesh):
    placed = (
        P("exp", None),
        P(None, "exp", None),
        P(None, "exp", "seq", None),
        P("exp"),
        P("seq", None),
        P("exp", None),
        P(),
        P(),
        P(),
        P(("seq", "exp"), None, None),
        P(("seq", "exp"), None, None),
        P(),
        P(),
        P(),
        P(),
        P(("seq", "exp"), None, None),
        P(("seq", "exp"), None, None),
    )
    return jax.shard_map(
        on_device,
        mesh=mesh,
        in_specs=placed,
        out_specs=(P("exp", None), P("exp", None)),
        check_vma=False,
    )
```
